256 devices in a mesh: blk: 128 (over x_lo, y, z, core), dp: 2 (over x_hi).
Axes of the slice: x: 4 (x_hi: 2, x_lo: 2; x = x_hi * 2 + x_lo), y: 4, z: 8, core: 2. Of those that a mesh axis runs over, the one named last changes fastest.
Arguments:
- fresh_rows: bfloat16 [131072, 2048], P(('blk', 'dp')), may hold values from -6 to 6
- older_rows: bfloat16 [131072, 2048], P(('blk', 'dp')), may hold values from -6 to 6
- older_cotangent: bfloat16 [131072, 2048], P(('blk', 'dp')), may hold values from -6 to 6
- weight_up: bfloat16 [2048, 5120], P(None, 'blk'), may hold values from -0.125 to 0.125
- weight_down: bfloat16 [5120, 2048], P('blk'), may hold values from -0.3125 to 0.3125
Outputs:
- fresh_output: bfloat16 [131072, 2048], P(('blk', 'dp'))
- older_input_grad: bfloat16 [131072, 2048], P(('blk', 'dp'))
- gradient_up: float32 [2048, 5120], P(None, 'blk')
- gradient_down: float32 [5120, 2048], P('blk')
The draws below stay inside these ranges and needn't reach their ends.
All inputs are finite; a program needn't handle non-finite values.
Results may differ from the reference program's by a relative error of at most 0.0049.
Values may be sent and summed in bfloat16 or wider, within the bound.
A program may use at most 192 MiB of HBM per device.

```python
import jax
import jax.numpy as jnp
from jax import lax

D = 2048
FF = 5120
TOK_DEV = 512
WINDOW = 8
SLICE = 40
WINHID = 320
TOKENS = 131072
N_BLK = 128
N_DP = 2


def levels(rng, shape, split, low, largest):
    level = 1.0
    for dim, shards_of in split:
        draws = jax.random.uniform(jax.random.fold_in(jax.random.fold_in(rng, 6), dim), (shards_of,), jnp.float32, low / len(split), largest / len(split))
        level = level * jnp.repeat(jnp.exp(draws), shape[dim] // shards_of).reshape((-1,) + (1,) * (len(shape) - 1 - dim))
    return level


def bell_draw(own_key, dims, width, bound, shards=(), kind=jnp.bfloat16):
    loudness = levels(own_key, dims, shards, -0.22, 0.18) if shards else 1.0
    values = jax.random.normal(own_key, dims, jnp.float32) * width * loudness
    return jnp.minimum(jnp.maximum(values, -bound), bound).astype(kind)


def setup_inputs(seed: int = 0) -> dict:
    arg_keys = jax.random.split(jax.random.key(seed), 6)
    fresh_rows = bell_draw(arg_keys[0], (TOKENS, D), 1.0, 6.0, ((0, 256),))
    older_rows = bell_draw(arg_keys[1], (TOKENS, D), 1.0, 6.0, ((0, 256),))
    older_cotangent = bell_draw(arg_keys[2], (TOKENS, D), 1.0, 6.0, ((0, 256),))
    weight_up = bell_draw(arg_keys[3], (D, FF), D ** -0.5, 0.125, ((1, 128),))
    weight_down = bell_draw(arg_keys[4], (FF, D), WINHID ** -0.5, 0.3125, ((0, 128),))
    return {"fresh_rows": fresh_rows, "older_rows": older_rows, "older_cotangent": older_cotangent, "weight_up": weight_up, "weight_down": weight_down}


def reference(fresh_rows, older_rows, older_cotangent, weight_up, weight_down):
    block_rows = N_DP * TOK_DEV
    fresh = fresh_rows.reshape(N_BLK, block_rows, D)
    older = older_rows.reshape(N_BLK, block_rows, D)
    cotangent = older_cotangent.reshape(N_BLK, block_rows, D)
    up_slices = weight_up.reshape(D, N_BLK, SLICE).transpose(1, 0, 2)
    down_slices = weight_down.reshape(N_BLK, SLICE, D)

    def per_block(inputs):
        device, fresh_block, older_block, cotangent_block = inputs
        output = jnp.zeros((block_rows, D), jnp.float32)
        backward = jnp.zeros((block_rows, D), jnp.float32)
        up_terms = []
        down_terms = []
        for offset in range(WINDOW):
            forward_index = (device - offset) % N_BLK
            up_piece = up_slices[forward_index]
            down_piece = down_slices[forward_index]
            fresh_pre = jnp.dot(fresh_block, up_piece, preferred_element_type=jnp.float32)
            fresh_act = jnp.square(jnp.maximum(fresh_pre, 0.0)).astype(jnp.bfloat16)
            output = output + jnp.dot(fresh_act, down_piece, preferred_element_type=jnp.float32)
            backward_index = (device + offset) % N_BLK
            up_back = up_slices[backward_index]
            down_back = down_slices[backward_index]
            older_pre = jnp.dot(older_block, up_back, preferred_element_type=jnp.float32)
            older_act = jnp.square(jnp.maximum(older_pre, 0.0)).astype(jnp.bfloat16)
            through = jnp.dot(cotangent_block, down_back.T, preferred_element_type=jnp.float32)
            grad_act = (through * 2.0 * jnp.maximum(older_pre, 0.0)).astype(jnp.bfloat16)
            backward = backward + jnp.dot(grad_act, up_back.T, preferred_element_type=jnp.float32)
            up_terms.append(jnp.dot(older_block.T, grad_act, preferred_element_type=jnp.float32))
            down_terms.append(jnp.dot(older_act.T, cotangent_block, preferred_element_type=jnp.float32))
        return (output.astype(jnp.bfloat16), backward.astype(jnp.bfloat16),
                jnp.stack(up_terms), jnp.stack(down_terms))

    devices = jnp.arange(N_BLK, dtype=jnp.int32)
    output, backward, up_terms, down_terms = lax.map(per_block, (devices, fresh, older, cotangent))
    up_total = jnp.zeros((N_BLK, D, SLICE), jnp.float32)
    down_total = jnp.zeros((N_BLK, SLICE, D), jnp.float32)
    for offset in range(WINDOW):
        up_total = up_total + jnp.roll(up_terms[:, offset], offset, axis=0)
        down_total = down_total + jnp.roll(down_terms[:, offset], offset, axis=0)
    factor = 1.0 / TOK_DEV
    gradient_up = (up_total * factor).transpose(1, 0, 2).reshape(D, FF)
    gradient_down = (down_total * factor).reshape(FF, D)
    return (output.reshape(TOKENS, D), backward.reshape(TOKENS, D), gradient_up, gradient_down)
```

```python
import functools

import jax
import jax.numpy as jnp
from jax import lax
from jax.experimental import pallas as pl
from jax.experimental.pallas import tpu as pltpu
from jax.sharding import PartitionSpec as P

MESH = pl.DeviceIdType.MESH
WINDOW = 8
REACH = WINDOW // 2
SLOTS = 2 * REACH + 1
SEAM = 32
COL_TILE = 512


def contract(left, right, dims):
    return lax.dot_general(left, right, (dims, ((), ())), preferred_element_type=jnp.float32)


def kernel(
    fresh_hbm, older_hbm, cot_hbm, up_ref, down_ref,
    out_hbm, igrad_hbm, grads_hbm,
    w, fresh, older, cot, grads_acc, act_t, gact_t, out_v, igrad_v, grads_v,
    sib_out, sib_in, x_out, x_in, x0_out, x0_in, z_out, z_in, z0_in,
    in_sem, out_sem,
    b_ss, b_rs, f_ss, f_rs, bs_ss, bs_rs, fs_ss, fs_rs,
    g_ss, g_rs, x_ss, x_rs, z_ss, z_rs, d_ss, d_rs,
):
    units, width = up_ref.shape
    packed = 2 * units
    pair = 2 * packed
    half = width // 2
    rows = older.shape[0]
    count = lax.axis_size("blk")
    me = lax.axis_index("blk")
    g = lax.axis_index("dp")
    k = lax.rem(me, 2)
    chip = me // 2
    ahead = lax.rem(me + 2, count)
    behind = lax.rem(me + count - 2, count)
    sibling = me + 1 - 2 * k
    other = 1 - g
    seam_up = lax.rem(chip, SEAM) == SEAM - 1
    seam_down = lax.rem(chip, SEAM) == 0

    barrier = pltpu.get_barrier_semaphore()
    peers = ((ahead, g), (behind, g), (sibling, g), (me, other), (ahead, other), (behind, other))
    for peer in peers:
        pl.semaphore_signal(barrier, inc=1, device_id=peer, device_id_type=MESH)

    loads = [
        pltpu.make_async_copy(src, dst, in_sem.at[i])
        for i, (src, dst) in enumerate(((older_hbm, older), (cot_hbm, cot), (fresh_hbm, fresh)))
    ]
    for load in loads:
        load.start()

    my_rows = pl.multiple_of(k * packed, 16)
    sib_rows = pl.multiple_of((1 - k) * packed, 16)
    my_cols = pl.multiple_of(g * half, 128)
    other_cols = pl.multiple_of(other * half, 128)
    w[REACH, pl.ds(my_rows, packed), :] = jnp.concatenate([up_ref[...], down_ref[...]], axis=0)
    w[0, 0:packed, :] = jnp.zeros((packed, width), w.dtype)
    w[SLOTS - 1, packed:pair, :] = jnp.zeros((packed, width), w.dtype)

    pl.semaphore_wait(barrier, len(peers))

    def remote(src, dst, send, recv, device):
        return pltpu.make_async_remote_copy(
            src_ref=src, dst_ref=dst, send_sem=send, recv_sem=recv,
            device_id=device, device_id_type=MESH,
        )

    def piece(slot, start, q):
        return w.at[slot, pl.ds(start, packed), pl.ds(q * half, half)]

    def send_back(h, q):
        group = jnp.where(seam_down, other, g) if q == 1 else g
        return remote(
            piece(REACH + h, my_rows, q), piece(REACH + h + 1, my_rows, q),
            b_ss.at[h, q], b_rs.at[h + 1, q], (behind, group),
        )

    def send_forth(h, q):
        group = jnp.where(seam_up, other, g) if q == 1 else g
        return remote(
            piece(REACH - h, my_rows, q), piece(REACH - h - 1, my_rows, q),
            f_ss.at[h, q], f_rs.at[h + 1, q], (ahead, group),
        )

    def recv_back(h, q):
        dst = piece(REACH + h, my_rows, q)
        return remote(dst, dst, b_ss.at[h, q], b_rs.at[h, q], (behind, g))

    def recv_forth(h, q):
        dst = piece(REACH - h, my_rows, q)
        return remote(dst, dst, f_ss.at[h, q], f_rs.at[h, q], (ahead, g))

    def share(slot, h, q, start, send, recv):
        ref = piece(slot, start, q)
        return remote(ref, ref, send.at[h, q], recv.at[h, q], (sibling, g))

    def share_back(h, q, start=my_rows):
        return share(REACH + h, h, q, start, bs_ss, bs_rs)

    def share_forth(h, q, start=my_rows):
        return share(REACH - h, h, q, start, fs_ss, fs_rs)

    def share_grads(h):
        return remote(sib_out.at[h], sib_in.at[h], g_ss.at[h], g_rs.at[h], (sibling, g))

    def swap(h):
        return remote(x_out.at[h], x_in.at[h], x_ss.at[h], x_rs.at[h], (me, other))

    def swap_last():
        return remote(x0_out, x0_in, x_ss.at[0], x_rs.at[0], (me, other))

    def carry(h):
        return remote(z_out.at[h], z_in.at[h - 1], z_ss.at[h], z_rs.at[h - 1], (ahead, g))

    def carry_last(cross):
        return remote(
            z_out.at[1], z0_in.at[:, pl.ds(my_cols, half)],
            (d_ss if cross else z_ss).at[1], (d_rs if cross else z_rs).at[0],
            (ahead, other if cross else g),
        )

    for q in range(2):
        share_back(0, q).start()
        send_back(0, q).start()
        send_forth(0, q).start()

    def valid(offset):
        return jnp.logical_and(offset >= 0, offset < WINDOW)

    def compute_back(h):
        block = w[REACH + h]
        pre = contract(block, older[...], ((1,), (1,)))
        through = contract(block, cot[...], ((1,), (1,)))
        blank = jnp.zeros((units, rows), jnp.float32)
        gact, act = [], []
        for p in range(2):
            keep = valid(2 * h + p - k)
            relu = jnp.maximum(pre[p * packed:p * packed + units], 0.0)
            thr = through[p * packed + units:(p + 1) * packed]
            gact += [jnp.where(keep, thr * 2.0 * relu, 0.0), blank]
            act += [blank, jnp.where(keep, jnp.square(relu), 0.0)]
        gact = jnp.concatenate(gact, axis=0).astype(jnp.bfloat16)
        act = jnp.concatenate(act, axis=0).astype(jnp.bfloat16)
        gact_t[h] = gact

        @pl.loop(0, width // COL_TILE)
        def _(t):
            cols = pl.ds(pl.multiple_of(t * COL_TILE, COL_TILE), COL_TILE)
            grads_acc[h, :, cols] = (
                contract(gact_t[h], older[:, cols], ((1,), (0,)))
                + contract(act, cot[:, cols], ((1,), (0,)))
            )

        sib_out[h] = grads_acc[h, pl.ds(sib_rows, packed), :].astype(jnp.bfloat16)

    def reduce_near(h):
        share_grads(h).wait_recv()
        mine = grads_acc.at[h, pl.ds(my_rows, packed)]
        mine[:, pl.ds(my_cols, half)] += sib_in[h, :, pl.ds(my_cols, half)].astype(jnp.float32)
        x_out[h] = (
            mine[:, pl.ds(other_cols, half)]
            + sib_in[h, :, pl.ds(other_cols, half)].astype(jnp.float32)
        ).astype(jnp.bfloat16)
        swap(h).start()

    def reduce_own():
        share_grads(0).wait_recv()
        x0_out[...] = (
            grads_acc[0, pl.ds(my_rows, packed), :] + sib_in[0].astype(jnp.float32)
        ).astype(jnp.bfloat16)
        swap_last().start()

    @pl.loop(0, REACH + 1)
    def _(h):
        @pl.when(h == 0)
        def _():
            loads[0].wait()
            loads[1].wait()

        @pl.when(h > 0)
        def _():
            for q in range(2):
                @pl.when(h <= REACH - k)
                def _():
                    recv_back(h, q).wait_recv()

                    @pl.when(h + 1 <= REACH - k)
                    def _():
                        send_back(h, q).start()

                    share_back(h, q).start()

                @pl.when(h <= REACH - 1 + k)
                def _():
                    recv_forth(h, q).wait_recv()

                    @pl.when(h + 1 <= REACH - 1 + k)
                    def _():
                        send_forth(h, q).start()

                    share_forth(h, q).start()

        @pl.when(h == 1)
        def _():
            reduce_own()

        @pl.when(h > 1)
        def _():
            reduce_near(h - 1)

        @pl.when(h <= REACH - 1 + k)
        def _():
            for q in range(2):
                share_back(h, q, sib_rows).wait_recv()
            compute_back(h)

            share_grads(h).start()

    def chain(h, first):
        swap(h).wait_recv()
        total = (
            grads_acc[h, pl.ds(my_rows, packed), pl.ds(my_cols, half)]
            + x_in[h].astype(jnp.float32)
        )
        if not first:
            carry(h + 1).wait_recv()
            total = total + z_in[h].astype(jnp.float32)
        z_out[h] = total.astype(jnp.bfloat16)
        if h == 1:
            carry_last(False).start()
            carry_last(True).start()
        else:
            carry(h).start()

    @pl.when(k == 0)
    def _():
        share_grads(REACH).wait_recv()
        grads_acc[REACH, 0:packed, pl.ds(my_cols, half)] = (
            sib_in[REACH, :, pl.ds(my_cols, half)].astype(jnp.float32)
        )
        x_out[REACH] = sib_in[REACH, :, pl.ds(other_cols, half)]
        swap(REACH).start()
        gact_t[REACH] = jnp.zeros((pair, rows), jnp.bfloat16)

    @pl.when(k == 1)
    def _():
        chain(REACH - 1, True)

    loads[2].wait()
    for q in range(2):
        pass

    @pl.loop(1, REACH + 1)
    def _(h):
        @pl.when(h <= REACH - k)
        def _():
            for q in range(2):
                share_forth(h, q, sib_rows).wait_recv()

    @pl.loop(0, REACH + 1)
    def _(s):
        pre = contract(w[s], fresh[...], ((1,), (1,)))
        blank = jnp.zeros((units, rows), jnp.float32)
        act = []
        for p in range(2):
            keep = valid(k - 2 * (s - REACH) - p)
            relu = jnp.maximum(pre[p * packed:p * packed + units], 0.0)
            act += [blank, jnp.where(keep, jnp.square(relu), 0.0)]
        act_t[s] = jnp.concatenate(act, axis=0).astype(jnp.bfloat16)

    @pl.when(k == 0)
    def _():
        chain(REACH, True)

    def finish(lhs_ref, first_slot, dst, dst_hbm, sem):
        lhs = lhs_ref[...].reshape((REACH + 1) * pair, rows).T

        @pl.loop(0, width // COL_TILE)
        def _(t):
            cols = pl.ds(pl.multiple_of(t * COL_TILE, COL_TILE), COL_TILE)
            right = w[first_slot:first_slot + REACH + 1, :, cols].reshape((REACH + 1) * pair, COL_TILE)
            dst[:, cols] = contract(lhs, right, ((1,), (0,))).astype(dst.dtype)

        pltpu.make_async_copy(dst, dst_hbm, sem).start()

    finish(act_t, 0, out_v, out_hbm, out_sem.at[0])

    @pl.when(k == 0)
    def _():
        chain(REACH - 1, False)

    finish(gact_t, REACH, igrad_v, igrad_hbm, out_sem.at[1])

    for h in range(REACH - 2, 0, -1):
        chain(h, False)

    swap_last().wait_recv()
    remote(
        z_out.at[1], z0_in.at[:, pl.ds(my_cols, half)], z_ss.at[1], z_rs.at[0], (ahead, g)
    ).wait_recv()
    remote(
        z_out.at[1], z0_in.at[:, pl.ds(other_cols, half)], d_ss.at[1], d_rs.at[0], (ahead, other)
    ).wait_recv()
    total = x0_out[...].astype(jnp.float32) + x0_in[...].astype(jnp.float32)
    grads_v[...] = (total + z0_in[...].astype(jnp.float32)) * (1.0 / rows)
    last = pltpu.make_async_copy(grads_v, grads_hbm, out_sem.at[2])
    last.start()

    for q in range(2):
        share_back(0, q).wait_send()
        send_back(0, q).wait_send()
        send_forth(0, q).wait_send()

    @pl.loop(1, REACH + 1)
    def _(h):
        @pl.when(h <= REACH - k)
        def _():
            for q in range(2):
                @pl.when(h + 1 <= REACH - k)
                def _():
                    send_back(h, q).wait_send()

                share_back(h, q).wait_send()

        @pl.when(h <= REACH - 1 + k)
        def _():
            for q in range(2):
                @pl.when(h + 1 <= REACH - 1 + k)
                def _():
                    send_forth(h, q).wait_send()

                share_forth(h, q).wait_send()

    for h in range(REACH):
        share_grads(h).wait_send()
    swap_last().wait_send()
    for h in range(1, REACH):
        swap(h).wait_send()
    carry_last(False).wait_send()
    carry_last(True).wait_send()
    for h in range(2, REACH):
        carry(h).wait_send()

    @pl.when(k == 1)
    def _():
        share_grads(REACH).wait_send()

    @pl.when(k == 0)
    def _():
        swap(REACH).wait_send()
        carry(REACH).wait_send()

    pltpu.make_async_copy(out_v, out_hbm, out_sem.at[0]).wait()
    pltpu.make_async_copy(igrad_v, igrad_hbm, out_sem.at[1]).wait()
    last.wait()


def per_device(fresh_rows, older_rows, older_cotangent, weight_up, weight_down):
    rows, width = fresh_rows.shape
    units = weight_up.shape[1]
    packed = 2 * units
    pair = 2 * packed
    half = width // 2
    bf16, f32 = jnp.bfloat16, jnp.float32
    hops = REACH + 1
    dma = pltpu.SemaphoreType.DMA
    out, igrad, grads = pl.pallas_call(
        kernel,
        out_shape=(
            jax.ShapeDtypeStruct((rows, width), bf16),
            jax.ShapeDtypeStruct((rows, width), bf16),
            jax.ShapeDtypeStruct((packed, width), f32),
        ),
        in_specs=[pl.BlockSpec(memory_space=pl.ANY)] * 3
        + [pl.BlockSpec(memory_space=pltpu.VMEM)] * 2,
        out_specs=[pl.BlockSpec(memory_space=pl.ANY)] * 3,
        scratch_shapes=[
            pltpu.VMEM((SLOTS, pair, width), bf16),
            pltpu.VMEM((rows, width), bf16),
            pltpu.VMEM((rows, width), bf16),
            pltpu.VMEM((rows, width), bf16),
            pltpu.VMEM((hops, pair, width), f32),
            pltpu.VMEM((hops, pair, rows), bf16),
            pltpu.VMEM((hops, pair, rows), bf16),
            pltpu.VMEM((rows, width), bf16),
            pltpu.VMEM((rows, width), bf16),
            pltpu.VMEM((packed, width), f32),
            pltpu.VMEM((hops, packed, width), bf16),
            pltpu.VMEM((hops, packed, width), bf16),
            pltpu.VMEM((hops, packed, half), bf16),
            pltpu.VMEM((hops, packed, half), bf16),
            pltpu.VMEM((packed, width), bf16),
            pltpu.VMEM((packed, width), bf16),
            pltpu.VMEM((hops, packed, half), bf16),
            pltpu.VMEM((hops, packed, half), bf16),
            pltpu.VMEM((packed, width), bf16),
            dma((3,)), dma((3,)),
        ]
        + [dma((hops, 2))] * 8
        + [dma((hops,))] * 8,
        compiler_params=pltpu.CompilerParams(
            collective_id=0, has_side_effects=True, vmem_limit_bytes=56 * 2**20
        ),
    )(fresh_rows, older_rows, older_cotangent, weight_up.T, weight_down)
    return out, igrad, grads[:units].T, grads[units:]


def solution(mesh):
    in_specs = (
        P(("blk", "dp"), None),
        P(("blk", "dp"), None),
        P(("blk", "dp"), None),
        P(None, "blk"),
        P("blk", None),
    )
    out_specs = (P(("blk", "dp"), None), P(("blk", "dp"), None), P(None, "blk"), P("blk", None))
    return jax.shard_map(
        per_device, mesh=mesh, in_specs=in_specs, out_specs=out_specs, check_vma=False
    )
```

```python
import jax
import jax.numpy as jnp
from jax import lax
from jax.experimental import pallas as pl
from jax.experimental.pallas import tpu as pltpu
from jax.sharding import PartitionSpec as P

MESH = pl.DeviceIdType.MESH
WINDOW = 8
REACH = WINDOW // 2
SLOTS = 2 * REACH + 1
SEAM = 32
COL_TILE = 512
CHUNKS = 4


def contract(left, right, dims):
    return lax.dot_general(left, right, (dims, ((), ())), preferred_element_type=jnp.float32)


def kernel(
    fresh_hbm, older_hbm, cot_hbm, up_hbm, down_hbm,
    out_hbm, igrad_hbm, gup_hbm, gdown_hbm,
    w, fresh, older, cot, up_v, down_v, grads_acc, act_t, gact_t, out_v, igrad_v, grads_v,
    sib_out, sib_in, x_out, x_in, x0_out, x0_in, z_out, z_in, z0_in, far_out, far_in,
    in_sem, out_sem,
    b_ss, b_rs, f_ss, f_rs, bs_ss, bs_rs, fs_ss, fs_rs,
    g_ss, g_rs, x0_ss, x0_rs,
    x_ss, x_rs, z_ss, z_rs, d_ss, d_rs, far_ss, far_rs,
):
    units, width = up_v.shape
    packed = 2 * units
    pair = 2 * packed
    half = width // 2
    chunk = half // CHUNKS
    rows = older.shape[0]
    count = lax.axis_size("blk")
    me = lax.axis_index("blk")
    g = lax.axis_index("dp")
    k = lax.rem(me, 2)
    chip = me // 2
    ahead = lax.rem(me + 2, count)
    behind = lax.rem(me + count - 2, count)
    sibling = me + 1 - 2 * k
    across = lax.rem(me + count + 2 * k - 1, count)
    other = 1 - g
    seam_up = lax.rem(chip, SEAM) == SEAM - 1
    seam_down = lax.rem(chip, SEAM) == 0

    barrier = pltpu.get_barrier_semaphore()
    peers = (
        (ahead, g), (behind, g), (sibling, g), (me, other),
        (ahead, other), (behind, other), (across, g), (across, other),
    )
    for peer in peers:
        pl.semaphore_signal(barrier, inc=1, device_id=peer, device_id_type=MESH)

    loads = [
        pltpu.make_async_copy(src, dst, in_sem.at[i])
        for i, (src, dst) in enumerate((
            (up_hbm, up_v), (down_hbm, down_v), (older_hbm, older), (cot_hbm, cot), (fresh_hbm, fresh),
        ))
    ]
    for load in loads:
        load.start()

    my_rows = pl.multiple_of(k * packed, 16)
    sib_rows = pl.multiple_of((1 - k) * packed, 16)
    my_cols = pl.multiple_of(g * half, 128)
    other_cols = pl.multiple_of(other * half, 128)
    nothing = jnp.zeros((packed, width), w.dtype)
    w[0, 0:packed, :] = nothing
    w[SLOTS - 1, packed:pair, :] = nothing

    @pl.when(k == 1)
    def _():
        w[0, packed:pair, :] = nothing

    @pl.when(k == 0)
    def _():
        w[SLOTS - 1, 0:packed, :] = nothing
        gact_t[REACH] = jnp.zeros((pair, rows), jnp.bfloat16)

    loads[0].wait()
    loads[1].wait()
    w[REACH, pl.ds(my_rows, packed), :] = jnp.concatenate([up_v[...], down_v[...]], axis=0)

    pl.semaphore_wait(barrier, len(peers))

    def remote(src, dst, send, recv, device):
        return pltpu.make_async_remote_copy(
            src_ref=src, dst_ref=dst, send_sem=send, recv_sem=recv,
            device_id=device, device_id_type=MESH,
        )

    def piece(slot, start, q):
        return w.at[slot, pl.ds(start, packed), pl.ds(q * half, half)]

    def send_back(h, q, device=behind):
        group = jnp.where(seam_down, other, g) if q == 1 else g
        return remote(
            piece(REACH + h, my_rows, q), piece(REACH + h + 1, my_rows, q),
            b_ss.at[h, q], b_rs.at[h + 1, q], (device, group),
        )

    def send_forth(h, q, device=ahead):
        group = jnp.where(seam_up, other, g) if q == 1 else g
        return remote(
            piece(REACH - h, my_rows, q), piece(REACH - h - 1, my_rows, q),
            f_ss.at[h, q], f_rs.at[h + 1, q], (device, group),
        )

    def recv_back(h, q, start=my_rows):
        dst = piece(REACH + h, start, q)
        return remote(dst, dst, b_ss.at[h, q], b_rs.at[h, q], (behind, g))

    def recv_forth(h, q, start=my_rows):
        dst = piece(REACH - h, start, q)
        return remote(dst, dst, f_ss.at[h, q], f_rs.at[h, q], (ahead, g))

    def share(slot, h, q, start, send, recv):
        ref = piece(slot, start, q)
        return remote(ref, ref, send.at[h, q], recv.at[h, q], (sibling, g))

    def share_back(h, q, start=my_rows):
        return share(REACH + h, h, q, start, bs_ss, bs_rs)

    def share_forth(h, q, start=my_rows):
        return share(REACH - h, h, q, start, fs_ss, fs_rs)

    def share_grads(h):
        return remote(sib_out.at[h], sib_in.at[h], g_ss.at[h], g_rs.at[h], (sibling, g))

    def swap(h, c):
        return remote(x_out.at[h, c], x_in.at[h, c], x_ss.at[h, c], x_rs.at[h, c], (me, other))

    def swap_last():
        return remote(x0_out, x0_in, x0_ss.at[0], x0_rs.at[0], (me, other))

    def carry(h, c):
        return remote(z_out.at[h, c], z_in.at[h - 1, c], z_ss.at[h, c], z_rs.at[h - 1, c], (ahead, g))

    def carry_last(c, part, cross):
        return remote(
            z_out.at[1, c], z0_in.at[part, c],
            (d_ss if cross else z_ss).at[1, c], (d_rs if cross else z_rs).at[0, c],
            (ahead, other if cross else g),
        )

    def far(c, cross):
        n = 1 if cross else 0
        return remote(
            far_out.at[n, c], far_in.at[n, c], far_ss.at[n, c], far_rs.at[n, c],
            (across, other if cross else g),
        )

    for q in range(2):
        send_back(0, q).start()
    for q in range(2):
        share_back(0, q).start()
        send_forth(0, q).start()

    def valid(offset):
        return jnp.logical_and(offset >= 0, offset < WINDOW)

    blank = jnp.zeros((units, rows), jnp.float32)

    def backward_acts(pre, through, keep):
        relu = jnp.maximum(pre, 0.0)
        gact = jnp.where(keep, through * 2.0 * relu, 0.0)
        return [gact, blank], [blank, jnp.where(keep, jnp.square(relu), 0.0)]

    def pack(parts):
        return jnp.concatenate(parts, axis=0).astype(jnp.bfloat16)

    def column_tile(t):
        return pl.ds(pl.multiple_of(t * COL_TILE, COL_TILE), COL_TILE)

    def compute_back(h):
        block = w[REACH + h]
        pre = contract(block, older[...], ((1,), (1,)))
        through = contract(block, cot[...], ((1,), (1,)))
        gact, act = [], []
        for p in range(2):
            first = p * packed
            one, two = backward_acts(
                pre[first:first + units], through[first + units:first + packed], valid(2 * h + p - k)
            )
            gact += one
            act += two
        gact_t[h] = pack(gact)
        act = pack(act)

        @pl.loop(0, width // COL_TILE)
        def _(t):
            cols = column_tile(t)
            grads_acc[h, :, cols] = (
                contract(gact_t[h], older[:, cols], ((1,), (0,)))
                + contract(act, cot[:, cols], ((1,), (0,)))
            )

        sib_out[h] = grads_acc[h, pl.ds(sib_rows, packed), :].astype(jnp.bfloat16)
        share_grads(h).start()

    def compute_far():
        block = w[SLOTS - 1, 0:packed, :]
        pre = contract(block, older[...], ((1,), (1,)))
        through = contract(block, cot[...], ((1,), (1,)))
        gact, act = backward_acts(pre[0:units], through[units:packed], True)
        gact, act = pack(gact), pack(act)
        gact_t[REACH] = jnp.concatenate([gact, jnp.zeros((packed, rows), jnp.bfloat16)], axis=0)
        for n in (1, 0):
            @pl.loop(0, half // COL_TILE)
            def _(t):
                cols = pl.ds(
                    pl.multiple_of((other_cols if n == 1 else my_cols) + t * COL_TILE, COL_TILE), COL_TILE
                )
                sums = (
                    contract(gact, older[:, cols], ((1,), (0,)))
                    + contract(act, cot[:, cols], ((1,), (0,)))
                ).astype(jnp.bfloat16)
                per = COL_TILE // chunk
                for i in range(per):
                    far_out[n, t * per + i] = sums[:, i * chunk:(i + 1) * chunk]
                    far(t * per + i, n == 1).start()

    def compute_forth(s):
        pre = contract(w[s], fresh[...], ((1,), (1,)))
        act = []
        for p in range(2):
            keep = valid(k - 2 * (s - REACH) - p)
            relu = jnp.maximum(pre[p * packed:p * packed + units], 0.0)
            act += [blank, jnp.where(keep, jnp.square(relu), 0.0)]
        act_t[s] = pack(act)

    def chunk_cols(start, c):
        return pl.ds(pl.multiple_of(start + c * chunk, chunk), chunk)

    def reduce_near(h):
        share_grads(h).wait_recv()

        @pl.loop(0, CHUNKS)
        def _(c):
            cols = chunk_cols(other_cols, c)
            x_out[h, c] = (
                grads_acc[h, pl.ds(my_rows, packed), cols] + sib_in[h, :, cols].astype(jnp.float32)
            ).astype(jnp.bfloat16)
            swap(h, c).start()

    def reduce_own():
        share_grads(0).wait_recv()
        x0_out[...] = (
            grads_acc[0, pl.ds(my_rows, packed), :] + sib_in[0].astype(jnp.float32)
        ).astype(jnp.bfloat16)
        swap_last().start()

    @pl.loop(0, REACH)
    def _(h):
        @pl.when(h == 0)
        def _():
            loads[2].wait()
            loads[3].wait()

        @pl.when(h > 0)
        def _():
            for q in range(2):
                recv_back(h, q).wait_recv()

                @pl.when(h + 1 < REACH)
                def _():
                    send_back(h, q).start()

                @pl.when(jnp.logical_and(h + 1 == REACH, k == 0))
                def _():
                    send_back(h, q, across).start()

                share_back(h, q).start()

                recv_forth(h, q).wait_recv()

                @pl.when(h + 1 < REACH)
                def _():
                    send_forth(h, q).start()

                @pl.when(jnp.logical_and(h + 1 == REACH, k == 1))
                def _():
                    send_forth(h, q, across).start()

                share_forth(h, q).start()

        @pl.when(h == 1)
        def _():
            reduce_own()

        @pl.when(h > 1)
        def _():
            reduce_near(h - 1)

        for q in range(2):
            share_back(h, q, sib_rows).wait_recv()
        compute_back(h)

        @pl.when(h == 0)
        def _():
            loads[4].wait()

        @pl.when(h > 0)
        def _():
            for q in range(2):
                share_forth(h, q, sib_rows).wait_recv()

        compute_forth(REACH - h)

    def chain(h, first):
        @pl.loop(0, CHUNKS)
        def _(c):
            cols = chunk_cols(my_cols, c)
            swap(h, c).wait_recv()
            total = (
                grads_acc[h, pl.ds(my_rows, packed), cols]
                + sib_in[h, :, cols].astype(jnp.float32)
                + x_in[h, c].astype(jnp.float32)
            )
            if not first:
                if h == REACH - 1:
                    far(c, True).wait_recv()
                    far(c, False).wait_recv()
                    total = total + far_in[0, c].astype(jnp.float32) + far_in[1, c].astype(jnp.float32)
                else:
                    carry(h + 1, c).wait_recv()
                    total = total + z_in[h, c].astype(jnp.float32)
            z_out[h, c] = total.astype(jnp.bfloat16)
            if h == 1:
                carry_last(c, g, False).start()
                carry_last(c, g, True).start()
            else:
                carry(h, c).start()

    def out_tiles(first, last):
        @pl.loop(first, last)
        def _(t):
            cols = column_tile(t)
            left = act_t[...].reshape((REACH + 1) * pair, rows)
            right = w[0:REACH + 1, :, cols].reshape((REACH + 1) * pair, COL_TILE)
            out_v[:, cols] = contract(left, right, ((0,), (0,))).astype(out_v.dtype)

    def igrad_tiles(first, last):
        @pl.loop(first, last)
        def _(t):
            cols = column_tile(t)
            left = gact_t[...].reshape((REACH + 1) * pair, rows)
            right = w[REACH:SLOTS, :, cols].reshape((REACH + 1) * pair, COL_TILE)
            igrad_v[:, cols] = contract(left, right, ((0,), (0,))).astype(igrad_v.dtype)

    reduce_near(REACH - 1)

    @pl.when(k == 1)
    def _():
        for q in range(2):
            recv_back(REACH, q, 0).wait_recv()
        compute_far()
        chain(REACH - 1, True)

    @pl.when(k == 0)
    def _():
        for q in range(2):
            recv_forth(REACH, q, packed).wait_recv()

    compute_forth(0)
    tiles = width // COL_TILE
    out_tiles(0, tiles)
    out_done = pltpu.make_async_copy(out_v, out_hbm, out_sem.at[0])
    out_done.start()

    @pl.when(k == 0)
    def _():
        chain(REACH - 1, False)

    igrad_tiles(0, tiles // 2)
    chain(2, False)
    igrad_tiles(tiles // 2, tiles)
    igrad_done = pltpu.make_async_copy(igrad_v, igrad_hbm, out_sem.at[1])
    igrad_done.start()
    chain(1, False)

    swap_last().wait_recv()
    for n in range(2):
        @pl.loop(0, CHUNKS)
        def _(c):
            part = other if n == 1 else g
            carry_last(c, part, n == 1).wait_recv()
            cols = chunk_cols(other_cols if n == 1 else my_cols, c)
            total = x0_out[:, cols].astype(jnp.float32) + x0_in[:, cols].astype(jnp.float32)
            grads_v[:, cols] = (total + z0_in[part, c].astype(jnp.float32)) * (1.0 / rows)

    last = [
        pltpu.make_async_copy(grads_v.at[0:units], gup_hbm, out_sem.at[2]),
        pltpu.make_async_copy(grads_v.at[units:packed], gdown_hbm, out_sem.at[3]),
    ]
    for copy in last:
        copy.start()

    @pl.loop(0, REACH)
    def _(h):
        share_grads(h).wait_send()
        for q in range(2):
            share_back(h, q).wait_send()

            @pl.when(jnp.logical_or(h + 1 < REACH, k == 0))
            def _():
                send_back(h, q).wait_send()

            @pl.when(jnp.logical_or(h + 1 < REACH, k == 1))
            def _():
                send_forth(h, q).wait_send()

            @pl.when(h > 0)
            def _():
                share_forth(h, q).wait_send()

    swap_last().wait_send()

    @pl.loop(0, CHUNKS)
    def _(c):
        carry_last(c, g, False).wait_send()
        carry_last(c, g, True).wait_send()
        for h in range(1, REACH):
            swap(h, c).wait_send()
        for h in range(2, REACH):
            carry(h, c).wait_send()

        @pl.when(k == 1)
        def _():
            far(c, False).wait_send()
            far(c, True).wait_send()

    out_done.wait()
    igrad_done.wait()
    for copy in last:
        copy.wait()


def per_device(fresh_rows, older_rows, older_cotangent, weight_up, weight_down):
    rows, width = fresh_rows.shape
    units = weight_up.shape[1]
    packed = 2 * units
    pair = 2 * packed
    chunk = width // 2 // CHUNKS
    bf16, f32 = jnp.bfloat16, jnp.float32
    dma = pltpu.SemaphoreType.DMA
    out, igrad, grad_up, grad_down = pl.pallas_call(
        kernel,
        out_shape=(
            jax.ShapeDtypeStruct((rows, width), bf16),
            jax.ShapeDtypeStruct((rows, width), bf16),
            jax.ShapeDtypeStruct((units, width), f32),
            jax.ShapeDtypeStruct((units, width), f32),
        ),
        in_specs=[pl.BlockSpec(memory_space=pl.ANY)] * 5,
        out_specs=[pl.BlockSpec(memory_space=pl.ANY)] * 4,
        scratch_shapes=[
            pltpu.VMEM((SLOTS, pair, width), bf16),
            pltpu.VMEM((rows, width), bf16),
            pltpu.VMEM((rows, width), bf16),
            pltpu.VMEM((rows, width), bf16),
            pltpu.VMEM((units, width), bf16),
            pltpu.VMEM((units, width), bf16),
            pltpu.VMEM((REACH, pair, width), f32),
            pltpu.VMEM((REACH + 1, pair, rows), bf16),
            pltpu.VMEM((REACH + 1, pair, rows), bf16),
            pltpu.VMEM((rows, width), bf16),
            pltpu.VMEM((rows, width), bf16),
            pltpu.VMEM((packed, width), f32),
            pltpu.VMEM((REACH, packed, width), bf16),
            pltpu.VMEM((REACH, packed, width), bf16),
            pltpu.VMEM((REACH, CHUNKS, packed, chunk), bf16),
            pltpu.VMEM((REACH, CHUNKS, packed, chunk), bf16),
            pltpu.VMEM((packed, width), bf16),
            pltpu.VMEM((packed, width), bf16),
            pltpu.VMEM((REACH, CHUNKS, packed, chunk), bf16),
            pltpu.VMEM((REACH, CHUNKS, packed, chunk), bf16),
            pltpu.VMEM((2, CHUNKS, packed, chunk), bf16),
            pltpu.VMEM((2, CHUNKS, packed, chunk), bf16),
            pltpu.VMEM((2, CHUNKS, packed, chunk), bf16),
            dma((5,)), dma((4,)),
        ]
        + [dma((REACH + 1, 2))] * 8
        + [dma((REACH,))] * 2
        + [dma((1,))] * 2
        + [dma((REACH, CHUNKS))] * 2
        + [dma((REACH, CHUNKS))] * 2
        + [dma((REACH, CHUNKS))] * 2
        + [dma((2, CHUNKS))] * 2,
        compiler_params=pltpu.CompilerParams(
            collective_id=0, has_side_effects=True, vmem_limit_bytes=56 * 2**20
        ),
    )(fresh_rows, older_rows, older_cotangent, weight_up.T, weight_down)
    return out, igrad, grad_up.T, grad_down


def solution(mesh):
    in_specs = (
        P(("blk", "dp"), None),
        P(("blk", "dp"), None),
        P(("blk", "dp"), None),
        P(None, "blk"),
        P("blk", None),
    )
    out_specs = (P(("blk", "dp"), None), P(("blk", "dp"), None), P(None, "blk"), P("blk", None))
    return jax.shard_map(
        per_device, mesh=mesh, in_specs=in_specs, out_specs=out_specs, check_vma=False
    )
```

```python
import jax
import jax.numpy as jnp
from jax import lax
from jax.experimental import pallas as pl
from jax.experimental.pallas import tpu as pltpu
from jax.sharding import PartitionSpec as P

MESH = pl.DeviceIdType.MESH
WINDOW = 8
REACH = WINDOW // 2
SLOTS = 2 * REACH + 1
SEAM = 32
COL_TILE = 512
CHUNKS = 4


def contract(left, right, dims):
    return lax.dot_general(left, right, (dims, ((), ())), preferred_element_type=jnp.float32)


def kernel(
    fresh_hbm, older_hbm, cot_hbm, up_hbm, down_hbm,
    out_v, igrad_v, gup_v, gdown_v,
    w, fresh, older, cot, up_v, down_v, grads_acc, act_t, gact_t,
    sib_out, sib_in, x_out, x_in, x0_out, x0_in, z_out, z_in, z0_in, far_out, far_in,
    in_sem,
    b_ss, b_rs, f_ss, f_rs, bs_ss, bs_rs, fs_ss, fs_rs,
    g_ss, g_rs, x0_ss, x0_rs,
    x_ss, x_rs, z_ss, z_rs, d_ss, d_rs, far_ss, far_rs,
):
    units, width = up_v.shape
    packed = 2 * units
    pair = 2 * packed
    half = width // 2
    chunk = half // CHUNKS
    rows = older.shape[0]
    count = lax.axis_size("blk")
    me = lax.axis_index("blk")
    g = lax.axis_index("dp")
    k = lax.rem(me, 2)
    chip = me // 2
    ahead = lax.rem(me + 2, count)
    behind = lax.rem(me + count - 2, count)
    sibling = me + 1 - 2 * k
    across = lax.rem(me + count + 2 * k - 1, count)
    other = 1 - g
    seam_up = lax.rem(chip, SEAM) == SEAM - 1
    seam_down = lax.rem(chip, SEAM) == 0

    barrier = pltpu.get_barrier_semaphore()
    peers = (
        (ahead, g), (behind, g), (sibling, g), (me, other),
        (ahead, other), (behind, other), (across, g), (across, other),
    )
    for peer in peers:
        pl.semaphore_signal(barrier, inc=1, device_id=peer, device_id_type=MESH)

    loads = [
        pltpu.make_async_copy(src, dst, in_sem.at[i])
        for i, (src, dst) in enumerate((
            (up_hbm, up_v), (down_hbm, down_v), (older_hbm, older), (cot_hbm, cot), (fresh_hbm, fresh),
        ))
    ]
    for load in loads:
        load.start()

    my_rows = pl.multiple_of(k * packed, 16)
    sib_rows = pl.multiple_of((1 - k) * packed, 16)
    my_cols = pl.multiple_of(g * half, 128)
    other_cols = pl.multiple_of(other * half, 128)
    nothing = jnp.zeros((packed, width), w.dtype)
    w[0, 0:packed, :] = nothing
    w[SLOTS - 1, packed:pair, :] = nothing

    @pl.when(k == 1)
    def _():
        w[0, packed:pair, :] = nothing

    @pl.when(k == 0)
    def _():
        w[SLOTS - 1, 0:packed, :] = nothing
        gact_t[REACH] = jnp.zeros((pair, rows), jnp.bfloat16)

    loads[0].wait()
    loads[1].wait()
    w[REACH, pl.ds(my_rows, packed), :] = jnp.concatenate([up_v[...], down_v[...]], axis=0)

    pl.semaphore_wait(barrier, len(peers))

    def remote(src, dst, send, recv, device):
        return pltpu.make_async_remote_copy(
            src_ref=src, dst_ref=dst, send_sem=send, recv_sem=recv,
            device_id=device, device_id_type=MESH,
        )

    def piece(slot, start, q):
        return w.at[slot, pl.ds(start, packed), pl.ds(q * half, half)]

    def send_back(h, q, device=behind):
        group = jnp.where(seam_down, other, g) if q == 1 else g
        return remote(
            piece(REACH + h, my_rows, q), piece(REACH + h + 1, my_rows, q),
            b_ss.at[h, q], b_rs.at[h + 1, q], (device, group),
        )

    def send_forth(h, q, device=ahead):
        group = jnp.where(seam_up, other, g) if q == 1 else g
        return remote(
            piece(REACH - h, my_rows, q), piece(REACH - h - 1, my_rows, q),
            f_ss.at[h, q], f_rs.at[h + 1, q], (device, group),
        )

    def recv_back(h, q, start=my_rows):
        dst = piece(REACH + h, start, q)
        return remote(dst, dst, b_ss.at[h, q], b_rs.at[h, q], (behind, g))

    def recv_forth(h, q, start=my_rows):
        dst = piece(REACH - h, start, q)
        return remote(dst, dst, f_ss.at[h, q], f_rs.at[h, q], (ahead, g))

    def share(slot, h, q, start, send, recv):
        ref = piece(slot, start, q)
        return remote(ref, ref, send.at[h, q], recv.at[h, q], (sibling, g))

    def share_back(h, q, start=my_rows):
        return share(REACH + h, h, q, start, bs_ss, bs_rs)

    def share_forth(h, q, start=my_rows):
        return share(REACH - h, h, q, start, fs_ss, fs_rs)

    def share_grads(h):
        return remote(sib_out.at[h], sib_in.at[h], g_ss.at[h], g_rs.at[h], (sibling, g))

    def swap(h, c):
        return remote(x_out.at[h, c], x_in.at[h, c], x_ss.at[h, c], x_rs.at[h, c], (me, other))

    def swap_last():
        return remote(x0_out, x0_in, x0_ss.at[0], x0_rs.at[0], (me, other))

    def carry(h, c):
        return remote(z_out.at[h, c], z_in.at[h - 1, c], z_ss.at[h, c], z_rs.at[h - 1, c], (ahead, g))

    def carry_last(c, part, cross):
        return remote(
            z_out.at[1, c], z0_in.at[part, c],
            (d_ss if cross else z_ss).at[1, c], (d_rs if cross else z_rs).at[0, c],
            (ahead, other if cross else g),
        )

    def far(c, cross):
        n = 1 if cross else 0
        return remote(
            far_out.at[n, c], far_in.at[n, c], far_ss.at[n, c], far_rs.at[n, c],
            (across, other if cross else g),
        )

    for q in range(2):
        send_back(0, q).start()
    for q in range(2):
        share_back(0, q).start()
        send_forth(0, q).start()

    def valid(offset):
        return jnp.logical_and(offset >= 0, offset < WINDOW)

    blank = jnp.zeros((units, rows), jnp.float32)

    def backward_acts(pre, through, keep):
        relu = jnp.maximum(pre, 0.0)
        gact = jnp.where(keep, through * 2.0 * relu, 0.0)
        return [gact, blank], [blank, jnp.where(keep, jnp.square(relu), 0.0)]

    def pack(parts):
        return jnp.concatenate(parts, axis=0).astype(jnp.bfloat16)

    def column_tile(t):
        return pl.ds(pl.multiple_of(t * COL_TILE, COL_TILE), COL_TILE)

    def compute_back(h):
        block = w[REACH + h]
        pre = contract(block, older[...], ((1,), (1,)))
        through = contract(block, cot[...], ((1,), (1,)))
        gact, act = [], []
        for p in range(2):
            first = p * packed
            one, two = backward_acts(
                pre[first:first + units], through[first + units:first + packed], valid(2 * h + p - k)
            )
            gact += one
            act += two
        gact_t[h] = pack(gact)
        act = pack(act)

        @pl.loop(0, width // COL_TILE)
        def _(t):
            cols = column_tile(t)
            grads_acc[h, :, cols] = (
                contract(gact_t[h], older[:, cols], ((1,), (0,)))
                + contract(act, cot[:, cols], ((1,), (0,)))
            )

        sib_out[h] = grads_acc[h, pl.ds(sib_rows, packed), :].astype(jnp.bfloat16)
        share_grads(h).start()

    def compute_far():
        block = w[SLOTS - 1, 0:packed, :]
        pre = contract(block, older[...], ((1,), (1,)))
        through = contract(block, cot[...], ((1,), (1,)))
        gact, act = backward_acts(pre[0:units], through[units:packed], True)
        gact, act = pack(gact), pack(act)
        gact_t[REACH] = jnp.concatenate([gact, jnp.zeros((packed, rows), jnp.bfloat16)], axis=0)
        for n in (1, 0):
            @pl.loop(0, half // COL_TILE)
            def _(t):
                cols = pl.ds(
                    pl.multiple_of((other_cols if n == 1 else my_cols) + t * COL_TILE, COL_TILE), COL_TILE
                )
                sums = (
                    contract(gact, older[:, cols], ((1,), (0,)))
                    + contract(act, cot[:, cols], ((1,), (0,)))
                ).astype(jnp.bfloat16)
                per = COL_TILE // chunk
                for i in range(per):
                    far_out[n, t * per + i] = sums[:, i * chunk:(i + 1) * chunk]
                    far(t * per + i, n == 1).start()

    def compute_forth(s):
        pre = contract(w[s], fresh[...], ((1,), (1,)))
        act = []
        for p in range(2):
            keep = valid(k - 2 * (s - REACH) - p)
            relu = jnp.maximum(pre[p * packed:p * packed + units], 0.0)
            act += [blank, jnp.where(keep, jnp.square(relu), 0.0)]
        act_t[s] = pack(act)

    def chunk_cols(start, c):
        return pl.ds(pl.multiple_of(start + c * chunk, chunk), chunk)

    def reduce_near(h):
        share_grads(h).wait_recv()

        @pl.loop(0, CHUNKS)
        def _(c):
            cols = chunk_cols(other_cols, c)
            x_out[h, c] = (
                grads_acc[h, pl.ds(my_rows, packed), cols] + sib_in[h, :, cols].astype(jnp.float32)
            ).astype(jnp.bfloat16)
            swap(h, c).start()

    def reduce_own():
        share_grads(0).wait_recv()
        x0_out[...] = (
            grads_acc[0, pl.ds(my_rows, packed), :] + sib_in[0].astype(jnp.float32)
        ).astype(jnp.bfloat16)
        swap_last().start()

    def pass_on(h, q):
        recv_back(h, q).wait_recv()

        @pl.when(h + 1 < REACH)
        def _():
            send_back(h, q).start()

        @pl.when(jnp.logical_and(h + 1 == REACH, k == 0))
        def _():
            send_back(h, q, across).start()

        share_back(h, q).start()
        recv_forth(h, q).wait_recv()

        @pl.when(h + 1 < REACH)
        def _():
            send_forth(h, q).start()

        @pl.when(jnp.logical_and(h + 1 == REACH, k == 1))
        def _():
            send_forth(h, q, across).start()

        share_forth(h, q).start()

    loads[2].wait()
    loads[3].wait()

    @pl.loop(0, REACH)
    def _(h):
        @pl.when(h > 0)
        def _():
            pass_on(h, 1)

        for q in range(2):
            share_back(h, q, sib_rows).wait_recv()
        compute_back(h)

        @pl.when(h + 1 < REACH)
        def _():
            pass_on(h + 1, 0)

        @pl.when(h == 0)
        def _():
            loads[4].wait()

        @pl.when(h > 0)
        def _():
            for q in range(2):
                share_forth(h, q, sib_rows).wait_recv()

        compute_forth(REACH - h)

        @pl.when(h == 0)
        def _():
            reduce_own()

        @pl.when(h > 0)
        def _():
            reduce_near(h)

    def chain(h, first):
        @pl.loop(0, CHUNKS)
        def _(c):
            cols = chunk_cols(my_cols, c)
            swap(h, c).wait_recv()
            total = (
                grads_acc[h, pl.ds(my_rows, packed), cols]
                + sib_in[h, :, cols].astype(jnp.float32)
                + x_in[h, c].astype(jnp.float32)
            )
            if not first:
                if h == REACH - 1:
                    far(c, True).wait_recv()
                    far(c, False).wait_recv()
                    total = total + far_in[0, c].astype(jnp.float32) + far_in[1, c].astype(jnp.float32)
                else:
                    carry(h + 1, c).wait_recv()
                    total = total + z_in[h, c].astype(jnp.float32)
            z_out[h, c] = total.astype(jnp.bfloat16)
            if h == 1:
                carry_last(c, g, False).start()
                carry_last(c, g, True).start()
            else:
                carry(h, c).start()

    def out_tiles(first, last):
        @pl.loop(first, last)
        def _(t):
            cols = column_tile(t)
            left = act_t[...].reshape((REACH + 1) * pair, rows)
            right = w[0:REACH + 1, :, cols].reshape((REACH + 1) * pair, COL_TILE)
            out_v[:, cols] = contract(left, right, ((0,), (0,))).astype(out_v.dtype)

    def igrad_tiles(first, last):
        @pl.loop(first, last)
        def _(t):
            cols = column_tile(t)
            left = gact_t[...].reshape((REACH + 1) * pair, rows)
            right = w[REACH:SLOTS, :, cols].reshape((REACH + 1) * pair, COL_TILE)
            igrad_v[:, cols] = contract(left, right, ((0,), (0,))).astype(igrad_v.dtype)

    @pl.when(k == 1)
    def _():
        for q in range(2):
            recv_back(REACH, q, 0).wait_recv()
        compute_far()
        chain(REACH - 1, True)

    @pl.when(k == 0)
    def _():
        for q in range(2):
            recv_forth(REACH, q, packed).wait_recv()

    compute_forth(0)
    tiles = width // COL_TILE
    out_tiles(0, tiles)

    @pl.when(k == 0)
    def _():
        chain(REACH - 1, False)

    igrad_tiles(0, tiles // 2)
    chain(2, False)
    igrad_tiles(tiles // 2, tiles)
    chain(1, False)

    swap_last().wait_recv()
    for n in range(2):
        @pl.loop(0, CHUNKS)
        def _(c):
            part = other if n == 1 else g
            carry_last(c, part, n == 1).wait_recv()
            cols = chunk_cols(other_cols if n == 1 else my_cols, c)
            total = x0_out[:, cols].astype(jnp.float32) + x0_in[:, cols].astype(jnp.float32)
            total = (total + z0_in[part, c].astype(jnp.float32)) * (1.0 / rows)
            gup_v[:, cols] = total[0:units]
            gdown_v[:, cols] = total[units:packed]

    @pl.loop(0, REACH)
    def _(h):
        share_grads(h).wait_send()
        for q in range(2):
            share_back(h, q).wait_send()

            @pl.when(jnp.logical_or(h + 1 < REACH, k == 0))
            def _():
                send_back(h, q).wait_send()

            @pl.when(jnp.logical_or(h + 1 < REACH, k == 1))
            def _():
                send_forth(h, q).wait_send()

            @pl.when(h > 0)
            def _():
                share_forth(h, q).wait_send()

    swap_last().wait_send()

    @pl.loop(0, CHUNKS)
    def _(c):
        carry_last(c, g, False).wait_send()
        carry_last(c, g, True).wait_send()
        for h in range(1, REACH):
            swap(h, c).wait_send()
        for h in range(2, REACH):
            carry(h, c).wait_send()

        @pl.when(k == 1)
        def _():
            far(c, False).wait_send()
            far(c, True).wait_send()


def per_device(fresh_rows, older_rows, older_cotangent, weight_up, weight_down):
    rows, width = fresh_rows.shape
    units = weight_up.shape[1]
    packed = 2 * units
    pair = 2 * packed
    chunk = width // 2 // CHUNKS
    bf16, f32 = jnp.bfloat16, jnp.float32
    dma = pltpu.SemaphoreType.DMA
    out, igrad, grad_up, grad_down = pl.pallas_call(
        kernel,
        out_shape=(
            pltpu.VMEM((rows, width), bf16),
            pltpu.VMEM((rows, width), bf16),
            pltpu.VMEM((units, width), f32),
            pltpu.VMEM((units, width), f32),
        ),
        in_specs=[pl.BlockSpec(memory_space=pl.ANY)] * 5,
        out_specs=[pl.BlockSpec(memory_space=pltpu.VMEM)] * 4,
        scratch_shapes=[
            pltpu.VMEM((SLOTS, pair, width), bf16),
            pltpu.VMEM((rows, width), bf16),
            pltpu.VMEM((rows, width), bf16),
            pltpu.VMEM((rows, width), bf16),
            pltpu.VMEM((units, width), bf16),
            pltpu.VMEM((units, width), bf16),
            pltpu.VMEM((REACH, pair, width), f32),
            pltpu.VMEM((REACH + 1, pair, rows), bf16),
            pltpu.VMEM((REACH + 1, pair, rows), bf16),
            pltpu.VMEM((REACH, packed, width), bf16),
            pltpu.VMEM((REACH, packed, width), bf16),
            pltpu.VMEM((REACH, CHUNKS, packed, chunk), bf16),
            pltpu.VMEM((REACH, CHUNKS, packed, chunk), bf16),
            pltpu.VMEM((packed, width), bf16),
            pltpu.VMEM((packed, width), bf16),
            pltpu.VMEM((REACH, CHUNKS, packed, chunk), bf16),
            pltpu.VMEM((REACH, CHUNKS, packed, chunk), bf16),
            pltpu.VMEM((2, CHUNKS, packed, chunk), bf16),
            pltpu.VMEM((2, CHUNKS, packed, chunk), bf16),
            pltpu.VMEM((2, CHUNKS, packed, chunk), bf16),
            dma((5,)),
        ]
        + [dma((REACH + 1, 2))] * 8
        + [dma((REACH,))] * 2
        + [dma((1,))] * 2
        + [dma((REACH, CHUNKS))] * 2
        + [dma((REACH, CHUNKS))] * 2
        + [dma((REACH, CHUNKS))] * 2
        + [dma((2, CHUNKS))] * 2,
        compiler_params=pltpu.CompilerParams(
            collective_id=0, has_side_effects=True, vmem_limit_bytes=56 * 2**20
        ),
    )(fresh_rows, older_rows, older_cotangent, weight_up.T, weight_down)
    return out, igrad, grad_up.T, grad_down


def solution(mesh):
    in_specs = (
        P(("blk", "dp"), None),
        P(("blk", "dp"), None),
        P(("blk", "dp"), None),
        P(None, "blk"),
        P("blk", None),
    )
    out_specs = (P(("blk", "dp"), None), P(("blk", "dp"), None), P(None, "blk"), P("blk", None))
    return jax.shard_map(
        per_device, mesh=mesh, in_specs=in_specs, out_specs=out_specs, check_vma=False
    )
```

```python
import jax
import jax.numpy as jnp
from jax import lax
from jax.experimental import pallas as pl
from jax.experimental.pallas import tpu as pltpu
from jax.sharding import PartitionSpec as P

MESH = pl.DeviceIdType.MESH
WINDOW = 8
REACH = WINDOW // 2
SLOTS = 2 * REACH + 1
SEAM = 32
COL_TILE = 512
CHUNKS = 4


def contract(left, right, dims):
    return lax.dot_general(left, right, (dims, ((), ())), preferred_element_type=jnp.float32)


def kernel(
    fresh_hbm, older_hbm, cot_hbm, up_hbm, down_hbm,
    out_v, igrad_v, gup_v, gdown_v,
    w, fresh, older, cot, up_v, down_v, grads_acc, act_t, gact_t,
    sib_out, sib_in, x_out, x_in, x0_out, x0_in, z_out, z_in, z0_in, far_out, far_in,
    in_sem,
    b_ss, b_rs, f_ss, f_rs, bs_ss, bs_rs, fs_ss, fs_rs,
    g_ss, g_rs, x0_ss, x0_rs,
    x_ss, x_rs, z_ss, z_rs, d_ss, d_rs, far_ss, far_rs,
):
    units, width = up_v.shape
    packed = 2 * units
    pair = 2 * packed
    half = width // 2
    chunk = half // CHUNKS
    rows = older.shape[0]
    count = lax.axis_size("blk")
    me = lax.axis_index("blk")
    g = lax.axis_index("dp")
    k = lax.rem(me, 2)
    chip = me // 2
    ahead = lax.rem(me + 2, count)
    behind = lax.rem(me + count - 2, count)
    sibling = me + 1 - 2 * k
    across = lax.rem(me + count + 2 * k - 1, count)
    other = 1 - g
    seam_up = lax.rem(chip, SEAM) == SEAM - 1
    seam_down = lax.rem(chip, SEAM) == 0
    late = lax.rem(chip, SEAM) < REACH

    barrier = pltpu.get_barrier_semaphore()
    peers = (
        (ahead, g), (behind, g), (sibling, g), (me, other),
        (ahead, other), (behind, other), (across, g), (across, other),
    )
    for peer in peers:
        pl.semaphore_signal(barrier, inc=1, device_id=peer, device_id_type=MESH)

    loads = [
        pltpu.make_async_copy(src, dst, in_sem.at[i])
        for i, (src, dst) in enumerate((
            (up_hbm, up_v), (down_hbm, down_v), (older_hbm, older), (cot_hbm, cot), (fresh_hbm, fresh),
        ))
    ]
    for load in loads:
        load.start()

    my_rows = pl.multiple_of(k * packed, 16)
    sib_rows = pl.multiple_of((1 - k) * packed, 16)
    my_cols = pl.multiple_of(g * half, 128)
    other_cols = pl.multiple_of(other * half, 128)
    nothing = jnp.zeros((packed, width), w.dtype)
    w[0, 0:packed, :] = nothing
    w[SLOTS - 1, packed:pair, :] = nothing

    @pl.when(k == 1)
    def _():
        w[0, packed:pair, :] = nothing

    @pl.when(k == 0)
    def _():
        w[SLOTS - 1, 0:packed, :] = nothing
        gact_t[REACH] = jnp.zeros((pair, rows), jnp.bfloat16)

    loads[0].wait()
    loads[1].wait()
    w[REACH, pl.ds(my_rows, packed), :] = jnp.concatenate([up_v[...], down_v[...]], axis=0)

    pl.semaphore_wait(barrier, len(peers))

    def remote(src, dst, send, recv, device):
        return pltpu.make_async_remote_copy(
            src_ref=src, dst_ref=dst, send_sem=send, recv_sem=recv,
            device_id=device, device_id_type=MESH,
        )

    def piece(slot, start, q):
        return w.at[slot, pl.ds(start, packed), pl.ds(q * half, half)]

    def send_back(h, q, device=behind):
        group = jnp.where(seam_down, other, g) if q == 1 else g
        return remote(
            piece(REACH + h, my_rows, q), piece(REACH + h + 1, my_rows, q),
            b_ss.at[h, q], b_rs.at[h + 1, q], (device, group),
        )

    def send_forth(h, q, device=ahead):
        group = jnp.where(seam_up, other, g) if q == 1 else g
        return remote(
            piece(REACH - h, my_rows, q), piece(REACH - h - 1, my_rows, q),
            f_ss.at[h, q], f_rs.at[h + 1, q], (device, group),
        )

    def recv_back(h, q, start=my_rows):
        dst = piece(REACH + h, start, q)
        return remote(dst, dst, b_ss.at[h, q], b_rs.at[h, q], (behind, g))

    def recv_forth(h, q, start=my_rows):
        dst = piece(REACH - h, start, q)
        return remote(dst, dst, f_ss.at[h, q], f_rs.at[h, q], (ahead, g))

    def share(slot, h, q, start, send, recv):
        ref = piece(slot, start, q)
        return remote(ref, ref, send.at[h, q], recv.at[h, q], (sibling, g))

    def share_back(h, q, start=my_rows):
        return share(REACH + h, h, q, start, bs_ss, bs_rs)

    def share_forth(h, q, start=my_rows):
        return share(REACH - h, h, q, start, fs_ss, fs_rs)

    def share_grads(h):
        return remote(sib_out.at[h], sib_in.at[h], g_ss.at[h], g_rs.at[h], (sibling, g))

    def swap(h, c):
        return remote(x_out.at[h, c], x_in.at[h, c], x_ss.at[h, c], x_rs.at[h, c], (me, other))

    def swap_last():
        return remote(x0_out, x0_in, x0_ss.at[0], x0_rs.at[0], (me, other))

    def carry(h, c):
        return remote(z_out.at[h, c], z_in.at[h - 1, c], z_ss.at[h, c], z_rs.at[h - 1, c], (ahead, g))

    def carry_last(c, part, cross):
        return remote(
            z_out.at[1, c], z0_in.at[part, c],
            (d_ss if cross else z_ss).at[1, c], (d_rs if cross else z_rs).at[0, c],
            (ahead, other if cross else g),
        )

    def far(c, cross):
        n = 1 if cross else 0
        return remote(
            far_out.at[n, c], far_in.at[n, c], far_ss.at[n, c], far_rs.at[n, c],
            (across, other if cross else g),
        )

    for q in range(2):
        send_back(0, q).start()
    for q in range(2):
        share_back(0, q).start()
        send_forth(0, q).start()

    def valid(offset):
        return jnp.logical_and(offset >= 0, offset < WINDOW)

    blank = jnp.zeros((units, rows), jnp.float32)

    def backward_acts(pre, through, keep):
        relu = jnp.maximum(pre, 0.0)
        gact = jnp.where(keep, through * 2.0 * relu, 0.0)
        return [gact, blank], [blank, jnp.where(keep, jnp.square(relu), 0.0)]

    def pack(parts):
        return jnp.concatenate(parts, axis=0).astype(jnp.bfloat16)

    def column_tile(t):
        return pl.ds(pl.multiple_of(t * COL_TILE, COL_TILE), COL_TILE)

    def compute_back(h):
        block = w[REACH + h]
        pre = contract(block, older[...], ((1,), (1,)))
        through = contract(block, cot[...], ((1,), (1,)))
        gact, act = [], []
        for p in range(2):
            first = p * packed
            one, two = backward_acts(
                pre[first:first + units], through[first + units:first + packed], valid(2 * h + p - k)
            )
            gact += one
            act += two
        gact_t[h] = pack(gact)
        act = pack(act)

        @pl.loop(0, width // COL_TILE)
        def _(t):
            cols = column_tile(t)
            grads_acc[h, :, cols] = (
                contract(gact_t[h], older[:, cols], ((1,), (0,)))
                + contract(act, cot[:, cols], ((1,), (0,)))
            )

        sib_out[h] = grads_acc[h, pl.ds(sib_rows, packed), :].astype(jnp.bfloat16)
        share_grads(h).start()

    def compute_far():
        block = w[SLOTS - 1, 0:packed, :]
        pre = contract(block, older[...], ((1,), (1,)))
        through = contract(block, cot[...], ((1,), (1,)))
        gact, act = backward_acts(pre[0:units], through[units:packed], True)
        gact, act = pack(gact), pack(act)
        gact_t[REACH] = jnp.concatenate([gact, jnp.zeros((packed, rows), jnp.bfloat16)], axis=0)
        for n in (1, 0):
            @pl.loop(0, half // COL_TILE)
            def _(t):
                cols = pl.ds(
                    pl.multiple_of((other_cols if n == 1 else my_cols) + t * COL_TILE, COL_TILE), COL_TILE
                )
                sums = (
                    contract(gact, older[:, cols], ((1,), (0,)))
                    + contract(act, cot[:, cols], ((1,), (0,)))
                ).astype(jnp.bfloat16)
                per = COL_TILE // chunk
                for i in range(per):
                    far_out[n, t * per + i] = sums[:, i * chunk:(i + 1) * chunk]
                    far(t * per + i, n == 1).start()

    def compute_forth(s):
        pre = contract(w[s], fresh[...], ((1,), (1,)))
        act = []
        for p in range(2):
            keep = valid(k - 2 * (s - REACH) - p)
            relu = jnp.maximum(pre[p * packed:p * packed + units], 0.0)
            act += [blank, jnp.where(keep, jnp.square(relu), 0.0)]
        act_t[s] = pack(act)

    def chunk_cols(start, c):
        return pl.ds(pl.multiple_of(start + c * chunk, chunk), chunk)

    def reduce_near(h):
        share_grads(h).wait_recv()

        @pl.loop(0, CHUNKS)
        def _(c):
            cols = chunk_cols(other_cols, c)
            x_out[h, c] = (
                grads_acc[h, pl.ds(my_rows, packed), cols] + sib_in[h, :, cols].astype(jnp.float32)
            ).astype(jnp.bfloat16)
            swap(h, c).start()

    def reduce_own():
        share_grads(0).wait_recv()
        x0_out[...] = (
            grads_acc[0, pl.ds(my_rows, packed), :] + sib_in[0].astype(jnp.float32)
        ).astype(jnp.bfloat16)
        swap_last().start()

    def pass_back(h, q):
        recv_back(h, q).wait_recv()

        @pl.when(h + 1 < REACH)
        def _():
            send_back(h, q).start()

        @pl.when(jnp.logical_and(h + 1 == REACH, k == 0))
        def _():
            send_back(h, q, across).start()

        share_back(h, q).start()

    def pass_forth(h, q):
        recv_forth(h, q).wait_recv()

        @pl.when(h + 1 < REACH)
        def _():
            send_forth(h, q).start()

        @pl.when(jnp.logical_and(h + 1 == REACH, k == 1))
        def _():
            send_forth(h, q, across).start()

        share_forth(h, q).start()

    def forth_ready(h):
        for q in range(2):
            share_forth(h, q, sib_rows).wait_recv()

    loads[2].wait()
    loads[3].wait()

    @pl.loop(0, REACH)
    def _(h):
        @pl.when(h > 0)
        def _():
            pass_back(h, 1)

        @pl.when(jnp.logical_and(h > 0, jnp.logical_not(late)))
        def _():
            pass_forth(h, 1)

        for q in range(2):
            share_back(h, q, sib_rows).wait_recv()
        compute_back(h)

        @pl.when(h + 1 < REACH)
        def _():
            pass_back(h + 1, 0)

        @pl.when(jnp.logical_and(h + 1 < REACH, jnp.logical_not(late)))
        def _():
            pass_forth(h + 1, 0)

        @pl.when(jnp.logical_and(h > 0, late))
        def _():
            pass_forth(h, 1)

        @pl.when(h == 1)
        def _():
            loads[4].wait()

        @pl.when(h > 1)
        def _():
            forth_ready(h - 1)

        @pl.when(h > 0)
        def _():
            compute_forth(REACH - h + 1)
            reduce_near(h)

        @pl.when(h == 0)
        def _():
            reduce_own()

        @pl.when(jnp.logical_and(h + 1 < REACH, late))
        def _():
            pass_forth(h + 1, 0)

    def chain(h, first):
        @pl.loop(0, CHUNKS)
        def _(c):
            cols = chunk_cols(my_cols, c)
            swap(h, c).wait_recv()
            total = (
                grads_acc[h, pl.ds(my_rows, packed), cols]
                + sib_in[h, :, cols].astype(jnp.float32)
                + x_in[h, c].astype(jnp.float32)
            )
            if not first:
                if h == REACH - 1:
                    far(c, True).wait_recv()
                    far(c, False).wait_recv()
                    total = total + far_in[0, c].astype(jnp.float32) + far_in[1, c].astype(jnp.float32)
                else:
                    carry(h + 1, c).wait_recv()
                    total = total + z_in[h, c].astype(jnp.float32)
            z_out[h, c] = total.astype(jnp.bfloat16)
            if h == 1:
                carry_last(c, g, False).start()
                carry_last(c, g, True).start()
            else:
                carry(h, c).start()

    def out_tiles(first, last):
        @pl.loop(first, last)
        def _(t):
            cols = column_tile(t)
            left = act_t[...].reshape((REACH + 1) * pair, rows)
            right = w[0:REACH + 1, :, cols].reshape((REACH + 1) * pair, COL_TILE)
            out_v[:, cols] = contract(left, right, ((0,), (0,))).astype(out_v.dtype)

    def igrad_tiles(first, last):
        @pl.loop(first, last)
        def _(t):
            cols = column_tile(t)
            left = gact_t[...].reshape((REACH + 1) * pair, rows)
            right = w[REACH:SLOTS, :, cols].reshape((REACH + 1) * pair, COL_TILE)
            igrad_v[:, cols] = contract(left, right, ((0,), (0,))).astype(igrad_v.dtype)

    @pl.when(k == 1)
    def _():
        for q in range(2):
            recv_back(REACH, q, 0).wait_recv()
        compute_far()
        chain(REACH - 1, True)

    tiles = width // COL_TILE

    @pl.when(k == 0)
    def _():
        igrad_tiles(0, tiles)
        chain(REACH - 1, False)

    chain(2, False)

    @pl.when(k == 1)
    def _():
        igrad_tiles(0, tiles)

    forth_ready(REACH - 1)
    compute_forth(1)
    chain(1, False)

    @pl.when(k == 0)
    def _():
        for q in range(2):
            recv_forth(REACH, q, packed).wait_recv()

    compute_forth(0)
    out_tiles(0, tiles)

    swap_last().wait_recv()
    for n in range(2):
        @pl.loop(0, CHUNKS)
        def _(c):
            part = other if n == 1 else g
            carry_last(c, part, n == 1).wait_recv()
            cols = chunk_cols(other_cols if n == 1 else my_cols, c)
            total = x0_out[:, cols].astype(jnp.float32) + x0_in[:, cols].astype(jnp.float32)
            total = (total + z0_in[part, c].astype(jnp.float32)) * (1.0 / rows)
            gup_v[:, cols] = total[0:units]
            gdown_v[:, cols] = total[units:packed]

    @pl.loop(0, REACH)
    def _(h):
        share_grads(h).wait_send()
        for q in range(2):
            share_back(h, q).wait_send()

            @pl.when(jnp.logical_or(h + 1 < REACH, k == 0))
            def _():
                send_back(h, q).wait_send()

            @pl.when(jnp.logical_or(h + 1 < REACH, k == 1))
            def _():
                send_forth(h, q).wait_send()

            @pl.when(h > 0)
            def _():
                share_forth(h, q).wait_send()

    swap_last().wait_send()

    @pl.loop(0, CHUNKS)
    def _(c):
        carry_last(c, g, False).wait_send()
        carry_last(c, g, True).wait_send()
        for h in range(1, REACH):
            swap(h, c).wait_send()
        for h in range(2, REACH):
            carry(h, c).wait_send()

        @pl.when(k == 1)
        def _():
            far(c, False).wait_send()
            far(c, True).wait_send()


def per_device(fresh_rows, older_rows, older_cotangent, weight_up, weight_down):
    rows, width = fresh_rows.shape
    units = weight_up.shape[1]
    packed = 2 * units
    pair = 2 * packed
    chunk = width // 2 // CHUNKS
    bf16, f32 = jnp.bfloat16, jnp.float32
    dma = pltpu.SemaphoreType.DMA
    out, igrad, grad_up, grad_down = pl.pallas_call(
        kernel,
        out_shape=(
            pltpu.VMEM((rows, width), bf16),
            pltpu.VMEM((rows, width), bf16),
            pltpu.VMEM((units, width), f32),
            pltpu.VMEM((units, width), f32),
        ),
        in_specs=[pl.BlockSpec(memory_space=pl.ANY)] * 5,
        out_specs=[pl.BlockSpec(memory_space=pltpu.VMEM)] * 4,
        scratch_shapes=[
            pltpu.VMEM((SLOTS, pair, width), bf16),
            pltpu.VMEM((rows, width), bf16),
            pltpu.VMEM((rows, width), bf16),
            pltpu.VMEM((rows, width), bf16),
            pltpu.VMEM((units, width), bf16),
            pltpu.VMEM((units, width), bf16),
            pltpu.VMEM((REACH, pair, width), f32),
            pltpu.VMEM((REACH + 1, pair, rows), bf16),
            pltpu.VMEM((REACH + 1, pair, rows), bf16),
            pltpu.VMEM((REACH, packed, width), bf16),
            pltpu.VMEM((REACH, packed, width), bf16),
            pltpu.VMEM((REACH, CHUNKS, packed, chunk), bf16),
            pltpu.VMEM((REACH, CHUNKS, packed, chunk), bf16),
            pltpu.VMEM((packed, width), bf16),
            pltpu.VMEM((packed, width), bf16),
            pltpu.VMEM((REACH, CHUNKS, packed, chunk), bf16),
            pltpu.VMEM((REACH, CHUNKS, packed, chunk), bf16),
            pltpu.VMEM((2, CHUNKS, packed, chunk), bf16),
            pltpu.VMEM((2, CHUNKS, packed, chunk), bf16),
            pltpu.VMEM((2, CHUNKS, packed, chunk), bf16),
            dma((5,)),
        ]
        + [dma((REACH + 1, 2))] * 8
        + [dma((REACH,))] * 2
        + [dma((1,))] * 2
        + [dma((REACH, CHUNKS))] * 2
        + [dma((REACH, CHUNKS))] * 2
        + [dma((REACH, CHUNKS))] * 2
        + [dma((2, CHUNKS))] * 2,
        compiler_params=pltpu.CompilerParams(
            collective_id=0, has_side_effects=True, vmem_limit_bytes=56 * 2**20
        ),
    )(fresh_rows, older_rows, older_cotangent, weight_up.T, weight_down)
    return out, igrad, grad_up.T, grad_down


def solution(mesh):
    in_specs = (
        P(("blk", "dp"), None),
        P(("blk", "dp"), None),
        P(("blk", "dp"), None),
        P(None, "blk"),
        P("blk", None),
    )
    out_specs = (P(("blk", "dp"), None), P(("blk", "dp"), None), P(None, "blk"), P("blk", None))
    return jax.shard_map(
        per_device, mesh=mesh, in_specs=in_specs, out_specs=out_specs, check_vma=False
    )
```

```python
import jax
import jax.numpy as jnp
from jax import lax
from jax.experimental import pallas as pl
from jax.experimental.pallas import tpu as pltpu
from jax.sharding import PartitionSpec as P

MESH = pl.DeviceIdType.MESH
WINDOW = 8
REACH = WINDOW // 2
SLOTS = 2 * REACH + 1
SEAM = 32
COL_TILE = 512
CHUNKS = 4


def contract(left, right, dims):
    return lax.dot_general(left, right, (dims, ((), ())), preferred_element_type=jnp.float32)


def kernel(
    fresh_hbm, older_hbm, cot_hbm, up_hbm, down_hbm,
    out_v, igrad_v, gup_v, gdown_v,
    w, fresh, older, cot, up_v, down_v, grads_acc, act_t, gact_t,
    sib_out, sib_in, x_out, x_in, x0_out, x0_in, z_out, z_in, z0_in, far_out, far_in,
    in_sem,
    b_ss, b_rs, f_ss, f_rs, bs_ss, bs_rs, fs_ss, fs_rs,
    g_ss, g_rs, x0_ss, x0_rs,
    x_ss, x_rs, z_ss, z_rs, d_ss, d_rs, far_ss, far_rs,
):
    units, width = up_v.shape
    packed = 2 * units
    pair = 2 * packed
    half = width // 2
    chunk = half // CHUNKS
    rows = older.shape[0]
    count = lax.axis_size("blk")
    me = lax.axis_index("blk")
    g = lax.axis_index("dp")
    k = lax.rem(me, 2)
    chip = me // 2
    ahead = lax.rem(me + 2, count)
    behind = lax.rem(me + count - 2, count)
    sibling = me + 1 - 2 * k
    across = lax.rem(me + count + 2 * k - 1, count)
    other = 1 - g
    seam_up = lax.rem(chip, SEAM) == SEAM - 1
    seam_down = lax.rem(chip, SEAM) == 0
    late = lax.rem(chip, SEAM) < REACH

    barrier = pltpu.get_barrier_semaphore()
    peers = (
        (ahead, g), (behind, g), (sibling, g), (me, other),
        (ahead, other), (behind, other), (across, g), (across, other),
    )
    for peer in peers:
        pl.semaphore_signal(barrier, inc=1, device_id=peer, device_id_type=MESH)

    loads = [
        pltpu.make_async_copy(src, dst, in_sem.at[i])
        for i, (src, dst) in enumerate((
            (up_hbm, up_v), (down_hbm, down_v), (older_hbm, older), (cot_hbm, cot), (fresh_hbm, fresh),
        ))
    ]
    for load in loads:
        load.start()

    my_rows = pl.multiple_of(k * packed, 16)
    sib_rows = pl.multiple_of((1 - k) * packed, 16)
    my_cols = pl.multiple_of(g * half, 128)
    other_cols = pl.multiple_of(other * half, 128)
    nothing = jnp.zeros((packed, width), w.dtype)
    w[0, 0:packed, :] = nothing
    w[SLOTS - 1, packed:pair, :] = nothing

    @pl.when(k == 1)
    def _():
        w[0, packed:pair, :] = nothing

    @pl.when(k == 0)
    def _():
        w[SLOTS - 1, 0:packed, :] = nothing
        gact_t[REACH] = jnp.zeros((pair, rows), jnp.bfloat16)

    loads[0].wait()
    loads[1].wait()
    w[REACH, pl.ds(my_rows, packed), :] = jnp.concatenate([up_v[...], down_v[...]], axis=0)

    pl.semaphore_wait(barrier, len(peers))

    def remote(src, dst, send, recv, device):
        return pltpu.make_async_remote_copy(
            src_ref=src, dst_ref=dst, send_sem=send, recv_sem=recv,
            device_id=device, device_id_type=MESH,
        )

    def piece(slot, start, q):
        return w.at[slot, pl.ds(start, packed), pl.ds(q * half, half)]

    def send_back(h, q, device=behind):
        group = jnp.where(seam_down, other, g) if q == 1 else g
        return remote(
            piece(REACH + h, my_rows, q), piece(REACH + h + 1, my_rows, q),
            b_ss.at[h, q], b_rs.at[h + 1, q], (device, group),
        )

    def send_forth(h, q, device=ahead):
        group = jnp.where(jnp.logical_and(seam_up, k == 1), other, g)
        return remote(
            piece(REACH - h, my_rows, q), piece(REACH - h - 1, my_rows, q),
            f_ss.at[h, q], f_rs.at[h + 1, q], (device, group),
        )

    def recv_back(h, q, start=my_rows):
        dst = piece(REACH + h, start, q)
        return remote(dst, dst, b_ss.at[h, q], b_rs.at[h, q], (behind, g))

    def recv_forth(h, q, start=my_rows):
        dst = piece(REACH - h, start, q)
        return remote(dst, dst, f_ss.at[h, q], f_rs.at[h, q], (ahead, g))

    def share(slot, h, q, start, send, recv):
        ref = piece(slot, start, q)
        return remote(ref, ref, send.at[h, q], recv.at[h, q], (sibling, g))

    def share_back(h, q, start=my_rows):
        return share(REACH + h, h, q, start, bs_ss, bs_rs)

    def share_forth(h, q, start=my_rows):
        return share(REACH - h, h, q, start, fs_ss, fs_rs)

    def share_grads(h):
        return remote(sib_out.at[h], sib_in.at[h], g_ss.at[h], g_rs.at[h], (sibling, g))

    def swap(h, c):
        return remote(x_out.at[h, c], x_in.at[h, c], x_ss.at[h, c], x_rs.at[h, c], (me, other))

    def swap_last():
        return remote(x0_out, x0_in, x0_ss.at[0], x0_rs.at[0], (me, other))

    def carry(h, c):
        return remote(z_out.at[h, c], z_in.at[h - 1, c], z_ss.at[h, c], z_rs.at[h - 1, c], (ahead, g))

    def carry_last(c, part, cross):
        return remote(
            z_out.at[1, c], z0_in.at[part, c],
            (d_ss if cross else z_ss).at[1, c], (d_rs if cross else z_rs).at[0, c],
            (ahead, other if cross else g),
        )

    def far(c, cross):
        n = 1 if cross else 0
        return remote(
            far_out.at[n, c], far_in.at[n, c], far_ss.at[n, c], far_rs.at[n, c],
            (across, other if cross else g),
        )

    for q in range(2):
        send_back(0, q).start()
    for q in range(2):
        share_back(0, q).start()
        send_forth(0, q).start()

    def valid(offset):
        return jnp.logical_and(offset >= 0, offset < WINDOW)

    blank = jnp.zeros((units, rows), jnp.float32)

    def backward_acts(pre, through, keep):
        relu = jnp.maximum(pre, 0.0)
        gact = jnp.where(keep, through * 2.0 * relu, 0.0)
        return [gact, blank], [blank, jnp.where(keep, jnp.square(relu), 0.0)]

    def pack(parts):
        return jnp.concatenate(parts, axis=0).astype(jnp.bfloat16)

    def column_tile(t):
        return pl.ds(pl.multiple_of(t * COL_TILE, COL_TILE), COL_TILE)

    def compute_back(h):
        block = w[REACH + h]
        pre = contract(block, older[...], ((1,), (1,)))
        through = contract(block, cot[...], ((1,), (1,)))
        gact, act = [], []
        for p in range(2):
            first = p * packed
            one, two = backward_acts(
                pre[first:first + units], through[first + units:first + packed], valid(2 * h + p - k)
            )
            gact += one
            act += two
        gact_t[h] = pack(gact)
        act = pack(act)

        @pl.loop(0, width // COL_TILE)
        def _(t):
            cols = column_tile(t)
            grads_acc[h, :, cols] = (
                contract(gact_t[h], older[:, cols], ((1,), (0,)))
                + contract(act, cot[:, cols], ((1,), (0,)))
            )

        sib_out[h] = grads_acc[h, pl.ds(sib_rows, packed), :].astype(jnp.bfloat16)
        share_grads(h).start()

    def compute_far():
        block = w[SLOTS - 1, 0:packed, :]
        pre = contract(block, older[...], ((1,), (1,)))
        through = contract(block, cot[...], ((1,), (1,)))
        gact, act = backward_acts(pre[0:units], through[units:packed], True)
        gact, act = pack(gact), pack(act)
        gact_t[REACH] = jnp.concatenate([gact, jnp.zeros((packed, rows), jnp.bfloat16)], axis=0)
        for n in (1, 0):
            @pl.loop(0, half // COL_TILE)
            def _(t):
                cols = pl.ds(
                    pl.multiple_of((other_cols if n == 1 else my_cols) + t * COL_TILE, COL_TILE), COL_TILE
                )
                sums = (
                    contract(gact, older[:, cols], ((1,), (0,)))
                    + contract(act, cot[:, cols], ((1,), (0,)))
                ).astype(jnp.bfloat16)
                per = COL_TILE // chunk
                for i in range(per):
                    far_out[n, t * per + i] = sums[:, i * chunk:(i + 1) * chunk]
                    far(t * per + i, n == 1).start()

    def compute_forth(s):
        pre = contract(w[s], fresh[...], ((1,), (1,)))
        act = []
        for p in range(2):
            keep = valid(k - 2 * (s - REACH) - p)
            relu = jnp.maximum(pre[p * packed:p * packed + units], 0.0)
            act += [blank, jnp.where(keep, jnp.square(relu), 0.0)]
        act_t[s] = pack(act)

    def chunk_cols(start, c):
        return pl.ds(pl.multiple_of(start + c * chunk, chunk), chunk)

    def reduce_near(h):
        share_grads(h).wait_recv()

        @pl.loop(0, CHUNKS)
        def _(c):
            cols = chunk_cols(other_cols, c)
            x_out[h, c] = (
                grads_acc[h, pl.ds(my_rows, packed), cols] + sib_in[h, :, cols].astype(jnp.float32)
            ).astype(jnp.bfloat16)
            swap(h, c).start()

    def reduce_own():
        share_grads(0).wait_recv()
        x0_out[...] = (
            grads_acc[0, pl.ds(my_rows, packed), :] + sib_in[0].astype(jnp.float32)
        ).astype(jnp.bfloat16)
        swap_last().start()

    def pass_back(h, q):
        recv_back(h, q).wait_recv()

        @pl.when(h + 1 < REACH)
        def _():
            send_back(h, q).start()

        @pl.when(jnp.logical_and(h + 1 == REACH, k == 0))
        def _():
            send_back(h, q, across).start()

        share_back(h, q).start()

    def pass_forth(h, q):
        recv_forth(h, q).wait_recv()

        @pl.when(h + 1 < REACH)
        def _():
            send_forth(h, q).start()

        @pl.when(jnp.logical_and(h + 1 == REACH, k == 1))
        def _():
            send_forth(h, q, across).start()

        share_forth(h, q).start()

    def forth_ready(h):
        for q in range(2):
            share_forth(h, q, sib_rows).wait_recv()

    loads[2].wait()
    loads[3].wait()

    @pl.loop(0, REACH)
    def _(h):
        @pl.when(h > 0)
        def _():
            pass_back(h, 1)

        @pl.when(jnp.logical_and(h > 0, jnp.logical_not(late)))
        def _():
            pass_forth(h, 1)

        for q in range(2):
            share_back(h, q, sib_rows).wait_recv()
        compute_back(h)

        @pl.when(h + 1 < REACH)
        def _():
            pass_back(h + 1, 0)

        @pl.when(jnp.logical_and(h + 1 < REACH, jnp.logical_not(late)))
        def _():
            pass_forth(h + 1, 0)

        @pl.when(jnp.logical_and(h > 0, late))
        def _():
            pass_forth(h, 1)

        @pl.when(h == 1)
        def _():
            loads[4].wait()

        @pl.when(h > 1)
        def _():
            forth_ready(h - 1)

        @pl.when(h > 0)
        def _():
            compute_forth(REACH - h + 1)
            reduce_near(h)

        @pl.when(h == 0)
        def _():
            reduce_own()

        @pl.when(jnp.logical_and(h + 1 < REACH, late))
        def _():
            pass_forth(h + 1, 0)

    def chain(h, first):
        @pl.loop(0, CHUNKS)
        def _(c):
            cols = chunk_cols(my_cols, c)
            swap(h, c).wait_recv()
            total = (
                grads_acc[h, pl.ds(my_rows, packed), cols]
                + sib_in[h, :, cols].astype(jnp.float32)
                + x_in[h, c].astype(jnp.float32)
            )
            if not first:
                if h == REACH - 1:
                    far(c, True).wait_recv()
                    far(c, False).wait_recv()
                    total = total + far_in[0, c].astype(jnp.float32) + far_in[1, c].astype(jnp.float32)
                else:
                    carry(h + 1, c).wait_recv()
                    total = total + z_in[h, c].astype(jnp.float32)
            z_out[h, c] = total.astype(jnp.bfloat16)
            if h == 1:
                carry_last(c, g, False).start()
                carry_last(c, g, True).start()
            else:
                carry(h, c).start()

    def out_tiles(first, last):
        @pl.loop(first, last)
        def _(t):
            cols = column_tile(t)
            left = act_t[...].reshape((REACH + 1) * pair, rows)
            right = w[0:REACH + 1, :, cols].reshape((REACH + 1) * pair, COL_TILE)
            out_v[:, cols] = contract(left, right, ((0,), (0,))).astype(out_v.dtype)

    def igrad_tiles(first, last):
        @pl.loop(first, last)
        def _(t):
            cols = column_tile(t)
            left = gact_t[...].reshape((REACH + 1) * pair, rows)
            right = w[REACH:SLOTS, :, cols].reshape((REACH + 1) * pair, COL_TILE)
            igrad_v[:, cols] = contract(left, right, ((0,), (0,))).astype(igrad_v.dtype)

    @pl.when(k == 1)
    def _():
        for q in range(2):
            recv_back(REACH, q, 0).wait_recv()
        compute_far()
        chain(REACH - 1, True)

    tiles = width // COL_TILE

    @pl.when(k == 0)
    def _():
        igrad_tiles(0, tiles)
        chain(REACH - 1, False)

    chain(2, False)

    @pl.when(k == 1)
    def _():
        igrad_tiles(0, tiles)

    forth_ready(REACH - 1)
    compute_forth(1)
    chain(1, False)

    @pl.when(k == 0)
    def _():
        for q in range(2):
            recv_forth(REACH, q, packed).wait_recv()

    compute_forth(0)
    out_tiles(0, tiles)

    swap_last().wait_recv()
    for n in range(2):
        @pl.loop(0, CHUNKS)
        def _(c):
            part = other if n == 1 else g
            carry_last(c, part, n == 1).wait_recv()
            cols = chunk_cols(other_cols if n == 1 else my_cols, c)
            total = x0_out[:, cols].astype(jnp.float32) + x0_in[:, cols].astype(jnp.float32)
            total = (total + z0_in[part, c].astype(jnp.float32)) * (1.0 / rows)
            gup_v[:, cols] = total[0:units]
            gdown_v[:, cols] = total[units:packed]

    @pl.loop(0, REACH)
    def _(h):
        share_grads(h).wait_send()
        for q in range(2):
            share_back(h, q).wait_send()

            @pl.when(jnp.logical_or(h + 1 < REACH, k == 0))
            def _():
                send_back(h, q).wait_send()

            @pl.when(jnp.logical_or(h + 1 < REACH, k == 1))
            def _():
                send_forth(h, q).wait_send()

            @pl.when(h > 0)
            def _():
                share_forth(h, q).wait_send()

    swap_last().wait_send()

    @pl.loop(0, CHUNKS)
    def _(c):
        carry_last(c, g, False).wait_send()
        carry_last(c, g, True).wait_send()
        for h in range(1, REACH):
            swap(h, c).wait_send()
        for h in range(2, REACH):
            carry(h, c).wait_send()

        @pl.when(k == 1)
        def _():
            far(c, False).wait_send()
            far(c, True).wait_send()


def per_device(fresh_rows, older_rows, older_cotangent, weight_up, weight_down):
    rows, width = fresh_rows.shape
    units = weight_up.shape[1]
    packed = 2 * units
    pair = 2 * packed
    chunk = width // 2 // CHUNKS
    bf16, f32 = jnp.bfloat16, jnp.float32
    dma = pltpu.SemaphoreType.DMA
    out, igrad, grad_up, grad_down = pl.pallas_call(
        kernel,
        out_shape=(
            pltpu.VMEM((rows, width), bf16),
            pltpu.VMEM((rows, width), bf16),
            pltpu.VMEM((units, width), f32),
            pltpu.VMEM((units, width), f32),
        ),
        in_specs=[pl.BlockSpec(memory_space=pl.ANY)] * 5,
        out_specs=[pl.BlockSpec(memory_space=pltpu.VMEM)] * 4,
        scratch_shapes=[
            pltpu.VMEM((SLOTS, pair, width), bf16),
            pltpu.VMEM((rows, width), bf16),
            pltpu.VMEM((rows, width), bf16),
            pltpu.VMEM((rows, width), bf16),
            pltpu.VMEM((units, width), bf16),
            pltpu.VMEM((units, width), bf16),
            pltpu.VMEM((REACH, pair, width), f32),
            pltpu.VMEM((REACH + 1, pair, rows), bf16),
            pltpu.VMEM((REACH + 1, pair, rows), bf16),
            pltpu.VMEM((REACH, packed, width), bf16),
            pltpu.VMEM((REACH, packed, width), bf16),
            pltpu.VMEM((REACH, CHUNKS, packed, chunk), bf16),
            pltpu.VMEM((REACH, CHUNKS, packed, chunk), bf16),
            pltpu.VMEM((packed, width), bf16),
            pltpu.VMEM((packed, width), bf16),
            pltpu.VMEM((REACH, CHUNKS, packed, chunk), bf16),
            pltpu.VMEM((REACH, CHUNKS, packed, chunk), bf16),
            pltpu.VMEM((2, CHUNKS, packed, chunk), bf16),
            pltpu.VMEM((2, CHUNKS, packed, chunk), bf16),
            pltpu.VMEM((2, CHUNKS, packed, chunk), bf16),
            dma((5,)),
        ]
        + [dma((REACH + 1, 2))] * 8
        + [dma((REACH,))] * 2
        + [dma((1,))] * 2
        + [dma((REACH, CHUNKS))] * 2
        + [dma((REACH, CHUNKS))] * 2
        + [dma((REACH, CHUNKS))] * 2
        + [dma((2, CHUNKS))] * 2,
        compiler_params=pltpu.CompilerParams(
            collective_id=0, has_side_effects=True, vmem_limit_bytes=56 * 2**20
        ),
    )(fresh_rows, older_rows, older_cotangent, weight_up.T, weight_down)
    return out, igrad, grad_up.T, grad_down


def solution(mesh):
    in_specs = (
        P(("blk", "dp"), None),
        P(("blk", "dp"), None),
        P(("blk", "dp"), None),
        P(None, "blk"),
        P("blk", None),
    )
    out_specs = (P(("blk", "dp"), None), P(("blk", "dp"), None), P(None, "blk"), P("blk", None))
    return jax.shard_map(
        per_device, mesh=mesh, in_specs=in_specs, out_specs=out_specs, check_vma=False
    )
```

```python
import jax
import jax.numpy as jnp
from jax import lax
from jax.experimental import pallas as pl
from jax.experimental.pallas import tpu as pltpu
from jax.sharding import PartitionSpec as P

MESH = pl.DeviceIdType.MESH
WINDOW = 8
REACH = WINDOW // 2
SLOTS = 2 * REACH + 1
SEAM = 32
COL_TILE = 512
CHUNKS = 4


def contract(left, right, dims):
    return lax.dot_general(left, right, (dims, ((), ())), preferred_element_type=jnp.float32)


def kernel(
    fresh_hbm, older_hbm, cot_hbm, up_hbm, down_hbm,
    out_v, igrad_v, gup_v, gdown_v,
    w, fresh, older, cot, up_v, down_v, grads_acc, act_t, gact_t,
    sib_out, sib_in, x_out, x_in, x0_out, x0_in, z_out, z_in, z0_in, far_out, far_in,
    in_sem,
    b_ss, b_rs, f_ss, f_rs, bs_ss, bs_rs, fs_ss, fs_rs,
    g_ss, g_rs, x0_ss, x0_rs,
    x_ss, x_rs, z_ss, z_rs, d_ss, d_rs, far_ss, far_rs,
):
    units, width = up_v.shape
    packed = 2 * units
    pair = 2 * packed
    half = width // 2
    chunk = half // CHUNKS
    rows = older.shape[0]
    count = lax.axis_size("blk")
    me = lax.axis_index("blk")
    g = lax.axis_index("dp")
    k = lax.rem(me, 2)
    chip = me // 2
    ahead = lax.rem(me + 2, count)
    behind = lax.rem(me + count - 2, count)
    sibling = me + 1 - 2 * k
    across = lax.rem(me + count + 2 * k - 1, count)
    other = 1 - g
    seam_up = lax.rem(chip, SEAM) == SEAM - 1
    seam_down = lax.rem(chip, SEAM) == 0
    late = lax.rem(chip, SEAM) < REACH

    barrier = pltpu.get_barrier_semaphore()
    peers = (
        (ahead, g), (behind, g), (sibling, g), (me, other),
        (ahead, other), (behind, other), (across, g), (across, other),
    )
    for peer in peers:
        pl.semaphore_signal(barrier, inc=1, device_id=peer, device_id_type=MESH)

    loads = [
        pltpu.make_async_copy(src, dst, in_sem.at[i])
        for i, (src, dst) in enumerate((
            (up_hbm, up_v), (down_hbm, down_v), (older_hbm, older), (cot_hbm, cot), (fresh_hbm, fresh),
        ))
    ]
    for load in loads:
        load.start()

    my_rows = pl.multiple_of(k * packed, 16)
    sib_rows = pl.multiple_of((1 - k) * packed, 16)
    my_cols = pl.multiple_of(g * half, 128)
    other_cols = pl.multiple_of(other * half, 128)
    nothing = jnp.zeros((packed, width), w.dtype)
    w[0, 0:packed, :] = nothing
    w[SLOTS - 1, packed:pair, :] = nothing

    @pl.when(k == 1)
    def _():
        w[0, packed:pair, :] = nothing
        act_t[0] = jnp.zeros((pair, rows), jnp.bfloat16)

    @pl.when(k == 0)
    def _():
        w[SLOTS - 1, 0:packed, :] = nothing
        gact_t[REACH] = jnp.zeros((pair, rows), jnp.bfloat16)

    loads[0].wait()
    loads[1].wait()
    w[REACH, pl.ds(my_rows, packed), :] = jnp.concatenate([up_v[...], down_v[...]], axis=0)

    pl.semaphore_wait(barrier, len(peers))

    def remote(src, dst, send, recv, device):
        return pltpu.make_async_remote_copy(
            src_ref=src, dst_ref=dst, send_sem=send, recv_sem=recv,
            device_id=device, device_id_type=MESH,
        )

    def piece(slot, start, q):
        return w.at[slot, pl.ds(start, packed), pl.ds(q * half, half)]

    def send_back(h, q, device=behind):
        group = jnp.where(seam_down, other, g) if q == 1 else g
        return remote(
            piece(REACH + h, my_rows, q), piece(REACH + h + 1, my_rows, q),
            b_ss.at[h, q], b_rs.at[h + 1, q], (device, group),
        )

    def send_forth(h, q, device=ahead):
        group = jnp.where(jnp.logical_and(seam_up, k == 1), other, g)
        return remote(
            piece(REACH - h, my_rows, q), piece(REACH - h - 1, my_rows, q),
            f_ss.at[h, q], f_rs.at[h + 1, q], (device, group),
        )

    def recv_back(h, q, start=my_rows):
        dst = piece(REACH + h, start, q)
        return remote(dst, dst, b_ss.at[h, q], b_rs.at[h, q], (behind, g))

    def recv_forth(h, q, start=my_rows):
        dst = piece(REACH - h, start, q)
        return remote(dst, dst, f_ss.at[h, q], f_rs.at[h, q], (ahead, g))

    def share(slot, h, q, start, send, recv):
        ref = piece(slot, start, q)
        return remote(ref, ref, send.at[h, q], recv.at[h, q], (sibling, g))

    def share_back(h, q, start=my_rows):
        return share(REACH + h, h, q, start, bs_ss, bs_rs)

    def share_forth(h, q, start=my_rows):
        return share(REACH - h, h, q, start, fs_ss, fs_rs)

    def share_grads(h):
        return remote(sib_out.at[h], sib_in.at[h], g_ss.at[h], g_rs.at[h], (sibling, g))

    def swap(h, c):
        return remote(x_out.at[h, c], x_in.at[h, c], x_ss.at[h, c], x_rs.at[h, c], (me, other))

    def swap_last():
        return remote(x0_out, x0_in, x0_ss.at[0], x0_rs.at[0], (me, other))

    def carry(h, c):
        return remote(z_out.at[h, c], z_in.at[h - 1, c], z_ss.at[h, c], z_rs.at[h - 1, c], (ahead, g))

    def carry_last(c, part, cross):
        return remote(
            z_out.at[1, c], z0_in.at[part, c],
            (d_ss if cross else z_ss).at[1, c], (d_rs if cross else z_rs).at[0, c],
            (ahead, other if cross else g),
        )

    def far(c, cross):
        n = 1 if cross else 0
        return remote(
            far_out.at[n, c], far_in.at[n, c], far_ss.at[n, c], far_rs.at[n, c],
            (across, other if cross else g),
        )

    for q in range(2):
        send_back(0, q).start()
    for q in range(2):
        share_back(0, q).start()
        send_forth(0, q).start()

    def valid(offset):
        return jnp.logical_and(offset >= 0, offset < WINDOW)

    blank = jnp.zeros((units, rows), jnp.float32)

    def backward_acts(pre, through, keep):
        relu = jnp.maximum(pre, 0.0)
        gact = jnp.where(keep, through * 2.0 * relu, 0.0)
        return [gact, blank], [blank, jnp.where(keep, jnp.square(relu), 0.0)]

    def pack(parts):
        return jnp.concatenate(parts, axis=0).astype(jnp.bfloat16)

    def column_tile(t):
        return pl.ds(pl.multiple_of(t * COL_TILE, COL_TILE), COL_TILE)

    def compute_back(h):
        block = w[REACH + h]
        pre = contract(block, older[...], ((1,), (1,)))
        through = contract(block, cot[...], ((1,), (1,)))
        gact, act = [], []
        for p in range(2):
            first = p * packed
            one, two = backward_acts(
                pre[first:first + units], through[first + units:first + packed], valid(2 * h + p - k)
            )
            gact += one
            act += two
        gact_t[h] = pack(gact)
        act = pack(act)

        @pl.loop(0, width // COL_TILE)
        def _(t):
            cols = column_tile(t)
            grads_acc[h, :, cols] = (
                contract(gact_t[h], older[:, cols], ((1,), (0,)))
                + contract(act, cot[:, cols], ((1,), (0,)))
            )

        sib_out[h] = grads_acc[h, pl.ds(sib_rows, packed), :].astype(jnp.bfloat16)
        share_grads(h).start()

    def compute_far():
        block = w[SLOTS - 1, 0:packed, :]
        pre = contract(block, older[...], ((1,), (1,)))
        through = contract(block, cot[...], ((1,), (1,)))
        gact, act = backward_acts(pre[0:units], through[units:packed], True)
        gact, act = pack(gact), pack(act)
        gact_t[REACH] = jnp.concatenate([gact, jnp.zeros((packed, rows), jnp.bfloat16)], axis=0)
        for n in (1, 0):
            @pl.loop(0, half // COL_TILE)
            def _(t):
                cols = pl.ds(
                    pl.multiple_of((other_cols if n == 1 else my_cols) + t * COL_TILE, COL_TILE), COL_TILE
                )
                sums = (
                    contract(gact, older[:, cols], ((1,), (0,)))
                    + contract(act, cot[:, cols], ((1,), (0,)))
                ).astype(jnp.bfloat16)
                per = COL_TILE // chunk
                for i in range(per):
                    far_out[n, t * per + i] = sums[:, i * chunk:(i + 1) * chunk]
                    far(t * per + i, n == 1).start()

    def compute_forth(s):
        pre = contract(w[s], fresh[...], ((1,), (1,)))
        act = []
        for p in range(2):
            keep = valid(k - 2 * (s - REACH) - p)
            relu = jnp.maximum(pre[p * packed:p * packed + units], 0.0)
            act += [blank, jnp.where(keep, jnp.square(relu), 0.0)]
        act_t[s] = pack(act)

    def chunk_cols(start, c):
        return pl.ds(pl.multiple_of(start + c * chunk, chunk), chunk)

    def reduce_near(h):
        share_grads(h).wait_recv()

        @pl.loop(0, CHUNKS)
        def _(c):
            cols = chunk_cols(other_cols, c)
            x_out[h, c] = (
                grads_acc[h, pl.ds(my_rows, packed), cols] + sib_in[h, :, cols].astype(jnp.float32)
            ).astype(jnp.bfloat16)
            swap(h, c).start()

    def reduce_own():
        share_grads(0).wait_recv()
        x0_out[...] = (
            grads_acc[0, pl.ds(my_rows, packed), :] + sib_in[0].astype(jnp.float32)
        ).astype(jnp.bfloat16)
        swap_last().start()

    def pass_back(h, q):
        recv_back(h, q).wait_recv()

        @pl.when(h + 1 < REACH)
        def _():
            send_back(h, q).start()

        @pl.when(jnp.logical_and(h + 1 == REACH, k == 0))
        def _():
            send_back(h, q, across).start()

        share_back(h, q).start()

    def pass_forth(h, q):
        recv_forth(h, q).wait_recv()

        @pl.when(h + 1 < REACH)
        def _():
            send_forth(h, q).start()

        @pl.when(jnp.logical_and(h + 1 == REACH, k == 1))
        def _():
            send_forth(h, q, across).start()

        share_forth(h, q).start()

    def forth_ready(h):
        for q in range(2):
            share_forth(h, q, sib_rows).wait_recv()

    loads[2].wait()
    loads[3].wait()

    @pl.loop(0, REACH)
    def _(h):
        @pl.when(h > 0)
        def _():
            pass_back(h, 1)

        @pl.when(jnp.logical_and(h > 0, jnp.logical_not(late)))
        def _():
            pass_forth(h, 1)

        for q in range(2):
            share_back(h, q, sib_rows).wait_recv()
        compute_back(h)

        @pl.when(h + 1 < REACH)
        def _():
            pass_back(h + 1, 0)

        @pl.when(jnp.logical_and(h + 1 < REACH, jnp.logical_not(late)))
        def _():
            pass_forth(h + 1, 0)

        @pl.when(jnp.logical_and(h > 0, late))
        def _():
            pass_forth(h, 1)

        @pl.when(h == 1)
        def _():
            loads[4].wait()

        @pl.when(h > 1)
        def _():
            forth_ready(h - 1)

        @pl.when(h > 0)
        def _():
            compute_forth(REACH - h + 1)
            reduce_near(h)

        @pl.when(h == 0)
        def _():
            reduce_own()

        @pl.when(jnp.logical_and(h + 1 < REACH, late))
        def _():
            pass_forth(h + 1, 0)

    def chain(h, first):
        @pl.loop(0, CHUNKS)
        def _(c):
            cols = chunk_cols(my_cols, c)
            swap(h, c).wait_recv()
            total = (
                grads_acc[h, pl.ds(my_rows, packed), cols]
                + sib_in[h, :, cols].astype(jnp.float32)
                + x_in[h, c].astype(jnp.float32)
            )
            if not first:
                if h == REACH - 1:
                    far(c, True).wait_recv()
                    far(c, False).wait_recv()
                    total = total + far_in[0, c].astype(jnp.float32) + far_in[1, c].astype(jnp.float32)
                else:
                    carry(h + 1, c).wait_recv()
                    total = total + z_in[h, c].astype(jnp.float32)
            z_out[h, c] = total.astype(jnp.bfloat16)
            if h == 1:
                carry_last(c, g, False).start()
                carry_last(c, g, True).start()
            else:
                carry(h, c).start()

    def out_tiles(first, last):
        @pl.loop(first, last)
        def _(t):
            cols = column_tile(t)
            left = act_t[...].reshape((REACH + 1) * pair, rows)
            right = w[0:REACH + 1, :, cols].reshape((REACH + 1) * pair, COL_TILE)
            out_v[:, cols] = contract(left, right, ((0,), (0,))).astype(out_v.dtype)

    def igrad_tiles(first, last):
        @pl.loop(first, last)
        def _(t):
            cols = column_tile(t)
            left = gact_t[...].reshape((REACH + 1) * pair, rows)
            right = w[REACH:SLOTS, :, cols].reshape((REACH + 1) * pair, COL_TILE)
            igrad_v[:, cols] = contract(left, right, ((0,), (0,))).astype(igrad_v.dtype)

    @pl.when(k == 1)
    def _():
        for q in range(2):
            recv_back(REACH, q, 0).wait_recv()
        compute_far()
        chain(REACH - 1, True)

    tiles = width // COL_TILE

    @pl.when(k == 0)
    def _():
        igrad_tiles(0, tiles)
        chain(REACH - 1, False)

    chain(2, False)

    @pl.when(k == 1)
    def _():
        igrad_tiles(0, tiles)

    forth_ready(REACH - 1)
    compute_forth(1)
    chain(1, False)

    @pl.when(k == 0)
    def _():
        for q in range(2):
            recv_forth(REACH, q, packed).wait_recv()
        compute_forth(0)

    out_tiles(0, tiles)

    swap_last().wait_recv()
    for n in range(2):
        @pl.loop(0, CHUNKS)
        def _(c):
            part = other if n == 1 else g
            carry_last(c, part, n == 1).wait_recv()
            cols = chunk_cols(other_cols if n == 1 else my_cols, c)
            total = x0_out[:, cols].astype(jnp.float32) + x0_in[:, cols].astype(jnp.float32)
            total = (total + z0_in[part, c].astype(jnp.float32)) * (1.0 / rows)
            gup_v[:, cols] = total[0:units]
            gdown_v[:, cols] = total[units:packed]

    @pl.loop(0, REACH)
    def _(h):
        share_grads(h).wait_send()
        for q in range(2):
            share_back(h, q).wait_send()

            @pl.when(jnp.logical_or(h + 1 < REACH, k == 0))
            def _():
                send_back(h, q).wait_send()

            @pl.when(jnp.logical_or(h + 1 < REACH, k == 1))
            def _():
                send_forth(h, q).wait_send()

            @pl.when(h > 0)
            def _():
                share_forth(h, q).wait_send()

    swap_last().wait_send()

    @pl.loop(0, CHUNKS)
    def _(c):
        carry_last(c, g, False).wait_send()
        carry_last(c, g, True).wait_send()
        for h in range(1, REACH):
            swap(h, c).wait_send()
        for h in range(2, REACH):
            carry(h, c).wait_send()

        @pl.when(k == 1)
        def _():
            far(c, False).wait_send()
            far(c, True).wait_send()


def per_device(fresh_rows, older_rows, older_cotangent, weight_up, weight_down):
    rows, width = fresh_rows.shape
    units = weight_up.shape[1]
    packed = 2 * units
    pair = 2 * packed
    chunk = width // 2 // CHUNKS
    bf16, f32 = jnp.bfloat16, jnp.float32
    dma = pltpu.SemaphoreType.DMA
    out, igrad, grad_up, grad_down = pl.pallas_call(
        kernel,
        out_shape=(
            pltpu.VMEM((rows, width), bf16),
            pltpu.VMEM((rows, width), bf16),
            pltpu.VMEM((units, width), f32),
            pltpu.VMEM((units, width), f32),
        ),
        in_specs=[pl.BlockSpec(memory_space=pl.ANY)] * 5,
        out_specs=[pl.BlockSpec(memory_space=pltpu.VMEM)] * 4,
        scratch_shapes=[
            pltpu.VMEM((SLOTS, pair, width), bf16),
            pltpu.VMEM((rows, width), bf16),
            pltpu.VMEM((rows, width), bf16),
            pltpu.VMEM((rows, width), bf16),
            pltpu.VMEM((units, width), bf16),
            pltpu.VMEM((units, width), bf16),
            pltpu.VMEM((REACH, pair, width), f32),
            pltpu.VMEM((REACH + 1, pair, rows), bf16),
            pltpu.VMEM((REACH + 1, pair, rows), bf16),
            pltpu.VMEM((REACH, packed, width), bf16),
            pltpu.VMEM((REACH, packed, width), bf16),
            pltpu.VMEM((REACH, CHUNKS, packed, chunk), bf16),
            pltpu.VMEM((REACH, CHUNKS, packed, chunk), bf16),
            pltpu.VMEM((packed, width), bf16),
            pltpu.VMEM((packed, width), bf16),
            pltpu.VMEM((REACH, CHUNKS, packed, chunk), bf16),
            pltpu.VMEM((REACH, CHUNKS, packed, chunk), bf16),
            pltpu.VMEM((2, CHUNKS, packed, chunk), bf16),
            pltpu.VMEM((2, CHUNKS, packed, chunk), bf16),
            pltpu.VMEM((2, CHUNKS, packed, chunk), bf16),
            dma((5,)),
        ]
        + [dma((REACH + 1, 2))] * 8
        + [dma((REACH,))] * 2
        + [dma((1,))] * 2
        + [dma((REACH, CHUNKS))] * 2
        + [dma((REACH, CHUNKS))] * 2
        + [dma((REACH, CHUNKS))] * 2
        + [dma((2, CHUNKS))] * 2,
        compiler_params=pltpu.CompilerParams(
            collective_id=0, has_side_effects=True, vmem_limit_bytes=56 * 2**20
        ),
    )(fresh_rows, older_rows, older_cotangent, weight_up.T, weight_down)
    return out, igrad, grad_up.T, grad_down


def solution(mesh):
    in_specs = (
        P(("blk", "dp"), None),
        P(("blk", "dp"), None),
        P(("blk", "dp"), None),
        P(None, "blk"),
        P("blk", None),
    )
    out_specs = (P(("blk", "dp"), None), P(("blk", "dp"), None), P(None, "blk"), P("blk", None))
    return jax.shard_map(
        per_device, mesh=mesh, in_specs=in_specs, out_specs=out_specs, check_vma=False
    )
```
